32 devices in a mesh: dp: 8 (over z, x), tensor: 4 (over y, core).
Axes of the slice: x: 2, y: 2, z: 4, core: 2. Of those that a mesh axis runs over, the one named last changes fastest.
Arguments:
- inputs: bfloat16 [16384, 768], P(('dp', 'tensor')), may hold values from -6 to 6
- w_qkv: bfloat16 [768, 3, 768], P(None, None, 'tensor'), may hold values from -0.21875 to 0.21875
- bias_query: float32 [768], P('tensor'), may hold values from -3 to 3
- bias_value: float32 [768], P('tensor'), may hold values from -3 to 3
- w_output: bfloat16 [768, 768], P('tensor'), may hold values from -0.875 to 0.875
- bias_output: float32 [768], replicated, may hold values from -2 to 2
- gain_attn: float32 [768], replicated, may hold values from 0.5 to 1.5
- shift_attn: float32 [768], replicated, may hold values from -2 to 2
- w_up: bfloat16 [768, 3072], P(None, 'tensor'), may hold values from -0.21875 to 0.21875
- bias_up: float32 [3072], P('tensor'), may hold values from -3 to 3
- w_down: bfloat16 [3072, 768], P('tensor'), may hold values from -0.21875 to 0.21875
- bias_down: float32 [768], replicated, may hold values from -2 to 2
- gain_ffn: float32 [768], replicated, may hold values from 0.5 to 1.5
- shift_ffn: float32 [768], replicated, may hold values from -2 to 2
- out_grad: bfloat16 [16384, 768], P(('dp', 'tensor')), may hold values from -6 to 6
- mlm_mask: int32 [16384], P(('dp', 'tensor')), may hold values 0 or 1
- span_doc: int32 [128], P(('dp', 'tensor')), may hold values from 0 to 31, as said below
- cls_grad: bfloat16 [32, 768], P('dp'), may hold values from -6 to 6
Outputs:
- mixed: bfloat16 [16384, 768], P(('dp', 'tensor'))
- input_grad: float32 [16384, 768], P(('dp', 'tensor'))
- grad_qkv: float32 [768, 3, 768], P(None, None, 'tensor')
- grad_bias_query: float32 [768], P('tensor')
- grad_bias_value: float32 [768], P('tensor')
- grad_output: float32 [768, 768], P('tensor')
- grad_bias_output: float32 [768], replicated
- grad_gain_attn: float32 [768], replicated
- grad_shift_attn: float32 [768], replicated
- grad_up: float32 [768, 3072], P(None, 'tensor')
- grad_bias_up: float32 [3072], P('tensor')
- grad_down: float32 [3072, 768], P('tensor')
- grad_bias_down: float32 [768], replicated
- grad_gain_ffn: float32 [768], replicated
- grad_shift_ffn: float32 [768], replicated
The draws below stay inside these ranges and needn't reach their ends.
Inputs may be any that keep to these rules, and one draw needn't show every extreme that they name: `span_doc`: Non-decreasing along the spans; the 16 spans of block b name documents b * 4 to (b + 1) * 4 - 1, the first of them naming the lowest and the last the highest.
All inputs are finite; a program needn't handle non-finite values. No bound on the sum of `mlm_mask` on one device may be relied on, other than what follows from the above.
Results may differ from the reference program's by a relative error of at most 0.015.
The reference program's roundings to bfloat16 on the way count: a program that leaves them out, or rounds other values in their place, can miss the bound.
Values may be sent and summed in bfloat16 or wider, within the bound.
No kernel may reach another device: no remote copies, remote signals or barrier semaphores. Data moves between devices by JAX's collectives and lax.ppermute only.
A program may use at most 128 MiB of HBM per device.

```python
import jax
import jax.numpy as jnp
from jax import lax

D = 768
HEADS = 12
FF = 3072
HEAD_DIM = 64
SPAN = 128
SPAN_DEV = 16
DOC_DEV = 4
SPANS = 128
TOKENS = 16384
DOCS = 32


def draw_span_doc(key, part):
    key = jax.random.fold_in(key, 7)
    blocks = SPANS // SPAN_DEV
    local = jax.random.randint(key, (blocks, SPAN_DEV), 0, DOC_DEV)
    local = jnp.sort(local, axis=1)
    local = local.at[:, 0].set(0).at[:, SPAN_DEV - 1].set(DOC_DEV - 1)
    base = jnp.arange(blocks, dtype=jnp.int32)[:, None] * DOC_DEV
    return (local + base).reshape(SPANS).astype(jnp.int32)


def with_ends(values, rng, low, largest):
    longest = values.shape.index(max(values.shape))
    spots = []
    for shift in (0, 1):
        where = [jax.random.randint(jax.random.fold_in(rng, axis), (), 0, length) for axis, length in enumerate(values.shape)]
        where[longest] = (where[longest] + shift) % values.shape[longest]
        spots.append(tuple(where))
    return values.at[spots[0]].set(low).at[spots[1]].set(largest)


def steps_of(stream_key, extent, shards, low, top_value):
    def one(position, shards_of):
        heights = jax.random.uniform(jax.random.fold_in(jax.random.fold_in(stream_key, 6), position), (shards_of,), jnp.float32, low / len(shards), top_value / len(shards))
        return jnp.repeat(jnp.exp(heights), extent[position] // shards_of).reshape((-1,) + (1,) * (len(extent) - position - 1))

    level = one(*shards[0])
    for cut in shards[1:]:
        level = level * one(*cut)
    return level


def scatter_about(own_key, shape, spread, most, split=(), kind=jnp.bfloat16):
    level = steps_of(own_key, shape, split, -0.22, 0.18) if split else 1.0
    values = jax.random.normal(own_key, shape, jnp.float32) * spread * level
    return jnp.minimum(jnp.maximum(values, -most), most).astype(kind)


def setup_inputs(seed: int = 0) -> dict:
    key_of = jax.random.split(jax.random.key(seed), 19)
    return {
        "inputs": scatter_about(key_of[0], (TOKENS, D), 1.0, 6.0, ((0, 32),)),
        "w_qkv": scatter_about(key_of[1], (D, 3, D), D ** -0.5, 0.21875, ((2, 4),)),
        "bias_query": scatter_about(key_of[2], (D,), 0.5, 3.0, ((0, 4),), jnp.float32),
        "bias_value": scatter_about(key_of[3], (D,), 0.5, 3.0, ((0, 4),), jnp.float32),
        "w_output": scatter_about(key_of[4], (D, D), (D // 16) ** -0.5, 0.875, ((0, 4),)),
        "bias_output": scatter_about(key_of[5], (D,), 0.3, 2.0, (), jnp.float32),
        "gain_attn": jnp.clip(1.0 + 0.1 * jax.random.normal(key_of[6], (D,), jnp.float32), 0.5, 1.5),
        "shift_attn": scatter_about(key_of[7], (D,), 0.3, 2.0, (), jnp.float32),
        "w_up": scatter_about(key_of[8], (D, FF), D ** -0.5, 0.21875, ((1, 4),)),
        "bias_up": scatter_about(key_of[9], (FF,), 0.5, 3.0, ((0, 4),), jnp.float32),
        "w_down": scatter_about(key_of[10], (FF, D), (FF // 4) ** -0.5, 0.21875, ((0, 4),)),
        "bias_down": scatter_about(key_of[11], (D,), 0.3, 2.0, (), jnp.float32),
        "gain_ffn": jnp.clip(1.0 + 0.1 * jax.random.normal(key_of[12], (D,), jnp.float32), 0.5, 1.5),
        "shift_ffn": scatter_about(key_of[13], (D,), 0.3, 2.0, (), jnp.float32),
        "out_grad": scatter_about(key_of[14], (TOKENS, D), 1.0, 6.0, ((0, 32),)),
        "mlm_mask": with_ends((jax.random.randint(key_of[15], (TOKENS,), 0, 20) < 3).astype(jnp.int32), jax.random.fold_in(key_of[15], 1), 0, 1),
        "span_doc": draw_span_doc(jax.random.fold_in(key_of[18], 71), 0),
        "cls_grad": scatter_about(key_of[17], (DOCS, D), 1.0, 6.0, ((0, 8),)),
    }


EPSILON = 1e-12
HIGH = lax.Precision.HIGHEST

@jax.custom_vjp
def low(v):
    return lax.optimization_barrier(v.astype(jnp.bfloat16)).astype(jnp.float32)

@jax.custom_vjp
def low_back(v):
    return v

def low_keep(v):
    return (low(v), None)

def low_pass(kept, grad):
    return (grad,)

def back_keep(v):
    return (v, None)

def back_low(kept, grad):
    return (low(grad),)
low.defvjp(low_keep, low_pass)
low_back.defvjp(back_keep, back_low)

def norm_rows(summed):
    centre = summed - lax.optimization_barrier(jnp.mean(summed, axis=-1, keepdims=True))
    return centre * lax.rsqrt(lax.optimization_barrier(jnp.mean(centre * centre, axis=-1, keepdims=True)) + EPSILON)

def layer_block(params, rows_in):
    w_qkv, bias_query, bias_value, w_output, bias_output, gain_attn, shift_attn, w_up, bias_up, w_down, bias_down, gain_ffn, shift_ffn = params
    count = rows_in.shape[0]
    shape4 = (count // SPAN, SPAN, HEADS, HEAD_DIM)
    projected = jnp.einsum('nd,dce->nce', rows_in, w_qkv, precision=HIGH)
    query = low(low_back(projected[:, 0] + bias_query)).reshape(shape4)
    keys = low(low_back(projected[:, 1])).reshape(shape4)
    values = low(low_back(projected[:, 2] + bias_value)).reshape(shape4)
    scale = 1.0 / HEAD_DIM ** 0.5
    scores = low_back(scale * jnp.einsum('sqhd,skhd->shqk', query, keys, precision=HIGH))
    weights = low(jax.nn.softmax(scores, axis=-1))
    context = jnp.einsum('shqk,skhd->sqhd', weights, values, precision=HIGH).reshape(count, D)
    context = low(low_back(context))
    attended = low_back(jnp.dot(context, w_output, precision=HIGH) + bias_output)
    first = norm_rows(rows_in + attended) * gain_attn + shift_attn
    upper = low_back(jnp.dot(low(first), w_up, precision=HIGH) + bias_up)
    active = low(jax.nn.gelu(upper, approximate=False))
    branch = low_back(jnp.dot(active, w_down, precision=HIGH) + bias_down)
    return norm_rows(first + branch) * gain_ffn + shift_ffn

def reference(inputs, w_qkv, bias_query, bias_value, w_output, bias_output, gain_attn, shift_attn, w_up, bias_up, w_down, bias_down, gain_ffn, shift_ffn, out_grad, mlm_mask, span_doc, cls_grad):
    params = tuple((p.astype(jnp.float32) for p in (w_qkv, bias_query, bias_value, w_output, bias_output, gain_attn, shift_attn, w_up, bias_up, w_down, bias_down, gain_ffn, shift_ffn)))
    group = 32 if SPANS % 32 == 0 else SPANS
    block_rows = group * SPAN

    def forward(weights_all, rows_all):
        blocks = rows_all.reshape(TOKENS // block_rows, block_rows, D)
        result = lax.map(lambda piece: jax.checkpoint(layer_block)(weights_all, piece), blocks)
        return result.reshape(TOKENS, D)
    outputs, pullback = jax.vjp(forward, params, inputs.astype(jnp.float32))
    weighting = jnp.where(mlm_mask == 1, 2.0, 0.5).astype(jnp.float32)
    upstream = out_grad.astype(jnp.float32) * weighting[:, None]
    cls_rows = cls_grad.astype(jnp.float32)[span_doc]
    upstream = upstream.reshape(SPANS, SPAN, D).at[:, 0, :].add(cls_rows).reshape(TOKENS, D)
    grads, input_grad = pullback(upstream)
    g_qkv, g_bias_query, g_bias_value, g_output, g_bias_output, g_gain_attn, g_shift_attn, g_up, g_bias_up, g_down, g_bias_down, g_gain_ffn, g_shift_ffn = grads
    return (outputs.astype(jnp.bfloat16), input_grad, g_qkv, g_bias_query, g_bias_value, g_output, g_bias_output, g_gain_attn, g_shift_attn, g_up, g_bias_up, g_down, g_bias_down, g_gain_ffn, g_shift_ffn)
```

```python
import functools
import math

import jax
import jax.numpy as jnp
from jax import lax
from jax.experimental import pallas as pl
from jax.experimental.pallas import tpu as pltpu
from jax.sharding import PartitionSpec as P

HEAD_DIM = 64
SPAN = 128
LANES = 128
EPSILON = 1e-12
SQRT_HALF = 0.7071067811865476
INV_ROOT_TWO_PI = 0.3989422804014327
SCALE = 1.0 / math.sqrt(HEAD_DIM)
BF = jnp.bfloat16
F32 = jnp.float32
MIB = 1 << 20

CORE, Y = 1, 2


def nn(a, b):
    return lax.dot_general(a, b, (((1,), (0,)), ((), ())), preferred_element_type=F32)


def nt(a, b):
    return lax.dot_general(a, b, (((1,), (1,)), ((), ())), preferred_element_type=F32)


def tn(a, b):
    return lax.dot_general(a, b, (((0,), (0,)), ((), ())), preferred_element_type=F32)


SCALARS = pl.BlockSpec(memory_space=pltpu.SMEM)
WHOLE = pl.BlockSpec(memory_space=pltpu.VMEM)


def call(body, index, args, out, scratch=(), vmem=40, name=None):
    return pl.pallas_call(
        body,
        out_shape=[jax.ShapeDtypeStruct(s, t) for s, t in out],
        in_specs=[SCALARS] + [WHOLE] * len(args),
        out_specs=[WHOLE] * len(out),
        scratch_shapes=list(scratch),
        compiler_params=pltpu.CompilerParams(vmem_limit_bytes=vmem * MIB),
        cost_estimate=pl.CostEstimate(flops=1000, bytes_accessed=0, transcendentals=0),
        name=name,
    )(index, *args)


def rows_at(start, size, unit=16):
    return pl.ds(pl.multiple_of(start, unit), size)


def gather_weights(index, halves, w):
    width = halves[0].shape[0] // 2
    pair = 2 * width
    for block in range(2):
        for order in range(2):
            ref = halves[2 * block + order]
            which = index[0] if order == 0 else 1 - index[0]
            for j in range(2):
                start = (2 * which + j) * pair + block * width
                w[rows_at(start, width), :] = ref[j * width : (j + 1) * width, :]


def probs_of(scores):
    expo = jnp.exp(scores - jnp.max(scores, axis=0, keepdims=True))
    return expo * (1.0 / jnp.sum(expo, axis=0, keepdims=True))


def two_heads(value):
    low = lax.broadcasted_iota(jnp.int32, value.shape, 1) < HEAD_DIM
    zero = jnp.zeros_like(value)
    return jnp.concatenate([jnp.where(low, value, zero), jnp.where(low, zero, value)], axis=0)


def of_two_heads(value):
    half = value.shape[0] // 2
    low = lax.broadcasted_iota(jnp.int32, (half, value.shape[1]), 1) < HEAD_DIM
    return jnp.where(low, value[:half], value[half:])


def norm_rows(summed):
    centre = summed - jnp.mean(summed, axis=-1, keepdims=True)
    factor = lax.rsqrt(jnp.mean(centre * centre, axis=-1, keepdims=True) + EPSILON)
    return centre * factor, factor


def norm_back(incoming, normed, factor, gain):
    scaled = incoming * gain
    return factor * (
        scaled
        - jnp.mean(scaled, axis=-1, keepdims=True)
        - normed * jnp.mean(scaled * normed, axis=-1, keepdims=True)
    )


def attend_body(last, index, x, w0a, w0b, w1a, w1b, bias, bias_col, acc, *rest):
    if last:
        norms, q, k, v, ctx, acc_out, second, first_low, w, vt = rest
    else:
        q, k, v, ctx, acc_out, w, vt = rest
    rows = x.shape[0]
    pair = w0a.shape[0]
    gather_weights(index, (w0a, w0b, w1a, w1b), w)
    query = (nt(x[...], w[:pair, :]) + bias[0:1, :]).astype(BF)
    q[...] = (query.astype(F32) * SCALE).astype(BF)
    k[...] = nt(x[...], w[pair : 2 * pair, :]).astype(BF)
    v[...] = (nt(x[...], w[2 * pair : 3 * pair, :]) + bias[1:2, :]).astype(BF)
    vt[...] = (nt(w[2 * pair : 3 * pair, :], x[...]) + bias_col[...]).astype(BF)

    def span(i, _):
        here = rows_at(i * SPAN, SPAN, SPAN)
        for tile in range(pair // LANES):
            cut = slice(tile * LANES, (tile + 1) * LANES)
            scores = nt(two_heads(k[here, cut]), q[here, cut])
            for h in range(2):
                probs = probs_of(scores[h * SPAN : (h + 1) * SPAN])
                own = slice(tile * LANES + h * HEAD_DIM, tile * LANES + (h + 1) * HEAD_DIM)
                ctx[own, here] = nn(vt[own, here], probs.astype(BF)).astype(BF)
        return 0

    lax.fori_loop(0, rows // SPAN, span, 0)
    total = acc[...] + tn(ctx[...], w[3 * pair :, :])
    acc_out[...] = total
    if last:
        normed, _ = norm_rows(total)
        first = normed * norms[0:1, :] + norms[1:2, :]
        first_low[...] = first.astype(BF)
        second[...] = first + norms[2:3, :]


def attend(index, x, halves, bias, bias_col, acc, norms=None):
    rows, dim = x.shape
    pair = halves[0].shape[0]
    last = norms is not None
    args = [x, *halves, bias, bias_col, acc] + ([norms] if last else [])
    out = [((rows, pair), BF)] * 3 + [((pair, rows), BF), ((rows, dim), F32)]
    if last:
        out += [((rows, dim), F32), ((rows, dim), BF)]
    return call(
        functools.partial(attend_body, last),
        index,
        args,
        out,
        [pltpu.VMEM((4 * pair, dim), BF), pltpu.VMEM((pair, rows), BF)],
        name="attend",
    )


def attend_back_body(index, q, k, v, ctx, grad, x, w0a, w0b, w1a, w1b, acc, *rest):
    qk0, qk1, vo0, vo1, sums, acc_out, w, kt, dc, dqt, dk, dv = rest
    rows = x.shape[0]
    pair = w0a.shape[0]
    width = pair // 2
    gather_weights(index, (w0a, w0b, w1a, w1b), w)
    kt[...] = nt(w[pair : 2 * pair, :], x[...]).astype(BF)
    dc[...] = nt(grad[...], w[3 * pair :, :]).astype(BF)

    def put(refs, place, value):
        value = value.astype(BF)
        refs[0][place] = value[:width]
        refs[1][place] = value[width:]

    put((vo0, vo1), 1 - index[1], nn(ctx[...], grad[...]))

    def span(i, _):
        here = rows_at(i * SPAN, SPAN, SPAN)
        for tile in range(pair // LANES):
            cut = slice(tile * LANES, (tile + 1) * LANES)
            query, grads = q[here, cut], dc[here, cut]
            scores = nt(two_heads(k[here, cut]), query)
            d_probs = nt(two_heads(v[here, cut]), grads)
            low_probs, low_scores = [], []
            for h in range(2):
                own = slice(h * SPAN, (h + 1) * SPAN)
                probs = probs_of(scores[own])
                inner = jnp.sum(d_probs[own] * probs, axis=0, keepdims=True)
                d_scores = (probs * (d_probs[own] - inner)).astype(BF)
                low_probs.append(probs.astype(BF))
                low_scores.append(d_scores)
                mine = slice(tile * LANES + h * HEAD_DIM, tile * LANES + (h + 1) * HEAD_DIM)
                dqt[mine, here] = (nn(kt[mine, here], d_scores) * SCALE).astype(BF)
            dk[here, cut] = of_two_heads(nn(jnp.concatenate(low_scores, axis=0), query)).astype(BF)
            dv[here, cut] = of_two_heads(nn(jnp.concatenate(low_probs, axis=0), grads)).astype(BF)
        return 0

    lax.fori_loop(0, rows // SPAN, span, 0)
    put((qk0, qk1), index[0], nn(dqt[...], x[...]))
    put((qk0, qk1), 1 - index[0], tn(dk[...], x[...]))
    put((vo0, vo1), index[1], tn(dv[...], x[...]))
    ones = jnp.ones((8, rows), BF)
    sums[0] = nt(ones, dqt[...])
    sums[1] = nn(ones, dv[...])
    acc_out[...] = (
        acc[...]
        + tn(dqt[...], w[:pair, :])
        + nn(dk[...], w[pair : 2 * pair, :])
        + nn(dv[...], w[2 * pair : 3 * pair, :])
    )


def attend_back(index, kept, grad, x, halves, acc):
    rows, dim = x.shape
    pair = halves[0].shape[0]
    part = ((2, pair // 2, dim), BF)
    return call(
        attend_back_body,
        index,
        [*kept, grad, x, *halves, acc],
        [part, part, part, part, ((2, 8, pair), F32), ((rows, dim), F32)],
        [pltpu.VMEM((4 * pair, dim), BF), pltpu.VMEM((pair, rows), BF)]
        + [pltpu.VMEM((rows, pair), BF), pltpu.VMEM((pair, rows), BF)]
        + [pltpu.VMEM((rows, pair), BF), pltpu.VMEM((rows, pair), BF)],
        name="attend_back",
    )


def feed_body(count, index, first, acc, *refs):
    bias, up, down = refs[:count], refs[count : 2 * count], refs[2 * count : 3 * count]
    active, slope = refs[3 * count : 4 * count], refs[4 * count : 5 * count]
    acc_out = refs[5 * count]
    total = acc[...]
    for i in range(count):
        step = min(up[i].shape[1], 384)
        for at in range(0, up[i].shape[1], step):
            cut = slice(at, at + step)
            upper = nn(first[...], up[i][:, cut]) + bias[i][:, cut]
            phi = 0.5 * (1.0 + lax.erf(upper * SQRT_HALF))
            act = (upper * phi).astype(BF)
            active[i][:, cut] = act
            slope[i][:, cut] = phi + upper * jnp.exp(-0.5 * upper * upper) * INV_ROOT_TWO_PI
            total = total + nn(act, down[i][cut, :])
    acc_out[...] = total


def feed(index, first, acc, bias, up, down):
    rows, dim = first.shape
    count = len(up)
    size = (rows, up[0].shape[1])
    out = call(
        functools.partial(feed_body, count),
        index,
        [first, acc, *bias, *up, *down],
        [(size, BF)] * count + [(size, F32)] * count + [((rows, dim), F32)],
        name="feed",
    )
    return out[:count], out[count : 2 * count], out[2 * count]


def feed_back_body(near, more, index, first, grad, acc, *refs):
    count = 1 if near else 2
    active, slope, up, down = (refs[i * count : (i + 1) * count] for i in range(4))
    refs = refs[4 * count :]
    if more:
        other, refs = refs[:4], refs[4:]
    g_up, g_down = refs[:2], refs[2:4]
    sums, acc_out = refs[4:]
    half = g_down[0].shape[0]
    ones = jnp.ones((8, first.shape[0]), BF)
    total = acc[...]
    for h in range(2):
        cut = slice(h * half, (h + 1) * half)
        if near:
            there = rows_at((index[0] if h == 0 else 1 - index[0]) * half, half, LANES)
            act, slp, w_up, w_down = (
                active[0][:, there],
                slope[0][:, there],
                up[0][:, there],
                down[0][there, :],
            )
        else:
            act, slp, w_up, w_down = active[h][...], slope[h][...], up[h][...], down[h][...]
        value = tn(act, grad[...])
        if more:
            value = value + other[2 + h][...].astype(F32)
        g_down[h][...] = value.astype(BF)
        d_upper = (nt(grad[...], w_down) * slp).astype(BF)
        sums[:, cut] = nn(ones, d_upper)
        for z in range(2):
            size = g_up[z].shape[0]
            there = rows_at((index[1] if z == 0 else 1 - index[1]) * size, size, LANES)
            value = tn(first[:, there], d_upper)
            if more:
                value = value + other[z][:, cut].astype(F32)
            g_up[z][:, cut] = value.astype(BF)
        total = total + nt(d_upper, w_up)
    acc_out[...] = total


def feed_back(index, first, grad, acc, active, slope, up, down, other=()):
    rows, dim = first.shape
    near = len(up) == 1
    units = sum(u.shape[1] for u in up)
    out = call(
        functools.partial(feed_back_body, near, bool(other)),
        index,
        [first, grad, acc, *active, *slope, *up, *down, *other],
        [((dim // 2, units), BF)] * 2
        + [((units // 2, dim), BF)] * 2
        + [((8, units), F32), ((rows, dim), F32)],
        name="feed_back",
    )
    return out[:4], out[4][0], out[5]


def turn_body(index, second, upstream, norms, mixed, d_second, low, sums):
    normed, factor = norm_rows(second[...])
    mixed[...] = (normed * norms[0:1, :] + norms[1:2, :]).astype(BF)
    incoming = upstream[...]
    grad = norm_back(incoming, normed, factor, norms[0:1, :])
    d_second[...] = grad
    low[...] = grad.astype(BF)
    sums[0:1, :] = jnp.sum(incoming * normed, axis=0, keepdims=True)
    sums[1:2, :] = jnp.sum(incoming, axis=0, keepdims=True)
    sums[2:3, :] = jnp.sum(grad.astype(BF).astype(F32), axis=0, keepdims=True)


def turn(index, second, upstream, norms):
    size = second.shape
    return call(
        turn_body,
        index,
        [second, upstream, norms],
        [(size, BF), (size, F32), (size, BF), ((3, size[1]), F32)],
        name="turn",
    )


def first_back_body(index, attended, incoming, norms, d_attn, low, sums):
    normed, factor = norm_rows(attended[...])
    grad = norm_back(incoming[...], normed, factor, norms[0:1, :])
    d_attn[...] = grad
    low[...] = grad.astype(BF)
    sums[0:1, :] = jnp.sum(incoming[...] * normed, axis=0, keepdims=True)
    sums[1:2, :] = jnp.sum(incoming[...], axis=0, keepdims=True)
    sums[2:3, :] = jnp.sum(grad.astype(BF).astype(F32), axis=0, keepdims=True)


def first_back(index, attended, incoming, norms):
    size = attended.shape
    return call(
        first_back_body,
        index,
        [attended, incoming, norms],
        [(size, F32), (size, BF), ((3, size[1]), F32)],
        name="first_back",
    )


def wide(value):
    return value.astype(F32)


def blocks(index, args, out, body, name="blocks"):
    def run(index, *refs):
        body(index, refs[: len(args)], refs[len(args) :])

    return call(run, index, args, out, vmem=16, name=name)


def sums(index, *groups):
    def body(_, ins, outs):
        at = 0
        for group, out in zip(groups, outs):
            total = wide(ins[at][...])
            for i in range(1, len(group)):
                total = total + wide(ins[at + i][...])
            out[...] = total.astype(BF)
            at += len(group)

    return blocks(
        index,
        [a for group in groups for a in group],
        [(group[0].shape, BF) for group in groups],
        body,
        name="sums",
    )


def split_sum(index, which, a, b):
    half = a.shape[0] // 2

    def body(index, ins, outs):
        for out, bit in zip(outs, (index[which], 1 - index[which])):
            there = rows_at(bit * half, half)
            out[...] = (wide(ins[0][there, :]) + wide(ins[1][there, :])).astype(BF)

    return blocks(index, [a, b], [((half, a.shape[1]), BF)] * 2, body, name="split_sum")


def join(index, which, own, other):
    half = own.shape[0]

    def body(index, ins, outs):
        for value, bit in zip(ins, (index[which], 1 - index[which])):
            outs[0][rows_at(bit * half, half), :] = value[...]

    return blocks(index, [own, other], [((2 * half, own.shape[1]), BF)], body, name="join")[0]


def swap(value, axis, bit):
    size = lax.axis_size(axis)
    return lax.ppermute(value, axis, [(i, i ^ bit) for i in range(size)])


class Order:
    def __init__(self, token):
        self.token = token

    def __call__(self, *values):
        self.token, *values = lax.optimization_barrier((self.token, *values))
        return values[0] if len(values) == 1 else values


def pick_half(value, index, axis=0):
    half = value.shape[axis] // 2
    return lax.dynamic_slice_in_dim(value, index * half, half, axis)


def local(
    inputs,
    w_qkv,
    bias_query,
    bias_value,
    w_output,
    bias_output,
    gain_attn,
    shift_attn,
    w_up,
    bias_up,
    w_down,
    bias_down,
    gain_ffn,
    shift_ffn,
    out_grad,
    mlm_mask,
    span_doc,
    cls_grad,
):
    rows, dim = inputs.shape
    width = w_qkv.shape[2]
    units = w_up.shape[1]
    half = units // 2
    dp = lax.axis_index("dp")
    bits = [1 << i for i in range(lax.axis_size("dp").bit_length() - 1)]
    ix = dp % 2
    index = jnp.stack([ix, (dp // bits[1]) % 2, (dp // bits[2]) % 2]).astype(jnp.int32)
    order = Order(bias_output)

    def core(value):
        return swap(value, "tensor", CORE)

    def over_y(value):
        return swap(value, "tensor", Y)

    def over(value, n):
        return swap(value, "dp", bits[n])

    own = jnp.concatenate([w_qkv.transpose(1, 2, 0).reshape(3 * width, dim), w_output], axis=0)
    attn = {0: (pick_half(own, ix), pick_half(own, 1 - ix))}
    attn_a = over_y(attn[0][0])
    attn[1] = tuple(core(t) for t in attn[0])
    small = [jnp.concatenate([bias_query, bias_value, bias_up])]
    small.append(core(small[0]))
    small.append(over_y(small[0]))

    def attend_biases(r):
        pairs = [
            jnp.concatenate([small[r + i][at : at + width] for i in range(2)])
            for at in (0, width)
        ]
        return jnp.stack(pairs), pairs[1][:, None]

    norms_attn = jnp.stack([gain_attn, shift_attn, bias_down])
    norms_ffn = jnp.stack([gain_ffn, shift_ffn])
    kept = {}
    attended = bias_output + inputs.astype(F32)

    near = order(*attn[0], *attn[1], attended, small[1])
    attn[0], attn[1], attended, small[1] = tuple(near[:2]), tuple(near[2:4]), near[4], near[5]
    *kept[0], attended = attend(index, inputs, attn[0] + attn[1], *attend_biases(0), attended)
    attended, attn_a, w_up, w_down = order(attended, attn_a, w_up, w_down)
    attn_b = over(attn_a, 0)
    far_a = core(attn_a)
    up_a = over_y(pick_half(w_up, ix, 1))
    down_send = pick_half(w_down, ix)
    up, down = {0: w_up}, {0: w_down}
    up[1], down[1] = core(w_up), core(w_down)
    small.append(core(small[2]))

    weighting = jnp.where(mlm_mask == 1, 2.0, 0.5).astype(F32)
    upstream = out_grad.astype(F32) * weighting[:, None]
    docs_here = cls_grad.shape[0]
    local_doc = span_doc - dp * docs_here
    picker = (local_doc[:, None] == jnp.arange(docs_here, dtype=jnp.int32)[None, :]).astype(F32)
    cls_rows = jnp.dot(picker, cls_grad.astype(F32), precision=lax.Precision.HIGHEST)
    upstream = (
        upstream.reshape(rows // SPAN, SPAN, dim).at[:, 0, :].add(cls_rows).reshape(rows, dim)
    )

    upstream, down_send, up_a = order(upstream, down_send, up_a)
    down_a = over_y(down_send)
    attn_b, far_a, up_a, small[2], small[3] = order(attn_b, far_a, up_a, small[2], small[3])
    far_b = core(attn_b)
    up_b = over(up_a, 0)
    up_far_a = core(up_a)
    far_b, attended = order(far_b, attended)
    attn[2], attn[3] = (attn_a, attn_b), (far_a, far_b)
    *kept[2], attended, second, first_low = attend(
        index, inputs, attn[2] + attn[3], *attend_biases(2), attended, norms_attn
    )

    bias_of = [t[2 * width :][None] for t in small]
    first_low, down_a, up[1], down[1] = order(first_low, down_a, up[1], down[1])
    down_b = over(down_a, 0)
    down_far_a = core(down_a)
    act_near, slope_near, second = feed(
        index, first_low, second, bias_of[:2], [up[0], up[1]], [down[0], down[1]]
    )
    second, up_b, up_far_a, down_far_a = order(second, up_b, up_far_a, down_far_a)
    up_far_b = core(up_b)
    bias_a = [pick_half(bias_of[r], ix, 1) for r in (2, 3)]
    bias_b = [pick_half(bias_of[r], 1 - ix, 1) for r in (2, 3)]
    act_a, slope_a, second = feed(
        index, first_low, second, bias_a, [up_a, up_far_a], [down_a, down_far_a]
    )
    second, down_b, up_far_b = order(second, down_b, up_far_b)
    down_far_b = order(core(down_b))
    act_b, slope_b, second = feed(
        index, first_low, second, bias_b, [up_b, up_far_b], [down_b, down_far_b]
    )
    mixed, d_second, branch_grad, sums_ffn = turn(index, second, upstream, norms_ffn)

    g_bias_up = {}

    def near_back(r, total, other=()):
        got, g_bias_up[r], total = feed_back(
            index, first_low, branch_grad, total, act_near[r : r + 1], slope_near[r : r + 1],
            [up[r]], [down[r]], other,
        )
        return got, total

    def far_back(r, total, other=()):
        ups = [up_a, up_b] if r == 2 else [up_far_a, up_far_b]
        downs = [down_a, down_b] if r == 2 else [down_far_a, down_far_b]
        got, g_bias_up[r], total = feed_back(
            index, first_low, branch_grad, total, [act_a[r - 2], act_b[r - 2]],
            [slope_a[r - 2], slope_b[r - 2]], ups, downs, other,
        )
        return got, total

    got, d_first = far_back(3, d_second)
    *got, d_first = order(*got, d_first)
    from_core = [core(t) for t in got]
    got, d_first = near_back(1, d_first)
    *got, d_first = order(*got, d_first)
    *from_core, d_first = order(*from_core, d_first)
    to_core = [core(t) for t in got]
    far, d_first = far_back(2, d_first, from_core)
    *far, d_first = order(*far, d_first)
    up_y = [over_y(far[1]), over_y(far[0])]
    down_x = [over(far[3], 0)]
    *to_core, d_first = order(*to_core, d_first)
    near, d_first = near_back(0, d_first, to_core)
    *near, d_first = order(*near, d_first)
    down_x.append(over(near[3], 0))

    d_attn, attended_grad, sums_attn = first_back(index, attended, d_first, norms_attn)
    g_query, g_value = {}, {}

    def attention_back(r, total):
        *got, sums_qv, total = attend_back(
            index, kept[r], attended_grad, inputs, attn[r] + attn[r + 1], total
        )
        for i in range(2):
            g_query[r + i] = sums_qv[0, 0, i * width : (i + 1) * width]
            g_value[r + i] = sums_qv[1, 0, i * width : (i + 1) * width]
        return got, total

    far_attn, input_grad = attention_back(2, d_attn)
    *far_attn, input_grad = order(*far_attn, input_grad)
    from_core = [core(far_attn[1]), core(far_attn[3])]
    near_attn, input_grad = attention_back(0, input_grad)
    *near_attn, input_grad = order(*near_attn, input_grad)
    to_core = [core(near_attn[1]), core(near_attn[3])]

    piece = ((width, dim), BF)

    def pair_sum(a, b, one):
        def body(_, ins, outs):
            for i in range(2):
                value = (wide(ins[0][i]) + wide(ins[1][i])).astype(BF)
                if one:
                    outs[0][i] = value
                else:
                    outs[i][...] = value

        return blocks(index, [a, b], [(a.shape, BF)] if one else [piece] * 2, body, name="pair_sum")

    *from_core, _ = order(*from_core, input_grad)
    (vo_far,) = pair_sum(far_attn[2], from_core[1], True)
    vo_y = over_y(order(vo_far))
    qk_far = order(*pair_sum(far_attn[0], from_core[0], False))
    up_y = order(*up_y)
    own_s, own_k = order(*sums(index, [near[1], up_y[0]], [near[0], up_y[1]]))
    up_z = over(own_s, 1)
    down_x = order(*down_x)
    down_far, down_near = order(*sums(index, [far[2], down_x[0]], [near[2], down_x[1]]))
    down_y = over_y(down_far)
    to_core = order(*to_core)
    qk_near = pair_sum(near_attn[0], to_core[0], False)

    def stack_body(_, ins, outs):
        for i in range(2):
            outs[0][i] = ins[i][...]

    qk_send = order(
        blocks(index, [qk_far[1], qk_near[1]], [((2, width, dim), BF)], stack_body, name="stack")[0]
    )
    qk_x = over(qk_send, 0)
    vo_near = pair_sum(near_attn[2], to_core[1], True)[0]

    vo_y, vo_near = order(vo_y, vo_near)
    vo_k, vo_s = order(*pair_sum(vo_near, vo_y, False))
    vo_z = over(vo_s, 1)
    up_z, own_k = order(up_z, own_k)

    def halves_body(_, ins, outs):
        for out, cut in zip(outs, (slice(0, half), slice(half, None))):
            out[...] = (wide(ins[0][:, cut]) + wide(ins[1][:, cut])).astype(BF)

    quarter = ((dim // 2, half), BF)
    up_k, up_s = order(*blocks(index, [own_k, up_z], [quarter] * 2, halves_body, name="up_halves"))
    up_x = over(up_s, 0)

    qk_x = order(qk_x)

    def qk_body(_, ins, outs):
        for i in range(2):
            outs[i][...] = (wide(ins[i][...]) + wide(ins[2][i])).astype(BF)

    qk_f, qk_n = order(*blocks(index, [qk_far[0], qk_near[0], qk_x], [piece] * 2, qk_body))
    qk_y = over_y(qk_f)
    vo_z = order(vo_z)
    (vo,) = order(*sums(index, [vo_k, vo_z])),
    vo_x = over(vo, 0)
    up_x = order(up_x)
    up_t = order(sums(index, [up_k, up_x])[0])
    up_z = over(up_t, 2)
    down_y = order(down_y)
    down_k, down_s = order(*split_sum(index, 1, down_near, down_y))
    down_z = over(down_s, 1)
    qk_y = order(qk_y)
    qk = order(sums(index, [qk_n, qk_y])[0])
    qk_z = over(qk, 1)
    down_z = order(down_z)
    down_k, down_s = order(*split_sum(index, 2, down_k, down_z))
    down_z = over(down_s, 2)
    vo_x = order(vo_x)
    vo = order(sums(index, [vo, vo_x])[0])
    up_z = order(up_z)
    up_t = order(sums(index, [up_t, up_z])[0])
    for n in range(3, len(bits)):
        up_t = sums(index, [up_t, over(up_t, n)])[0]
    up_x = over(up_t, 0)
    down_z = order(down_z)
    down = order(sums(index, [down_k, down_z])[0])
    for n in range(3, len(bits)):
        down = sums(index, [down, over(down, n)])[0]
    down_z = over(down, 2)
    vo_z = over(vo, 2)
    qk_z = order(qk_z)
    qk = order(sums(index, [qk, qk_z])[0])
    up_x = order(up_x)

    def side_body(_, ins, outs):
        for i in range(2):
            outs[0][:, i * half : (i + 1) * half] = ins[i][...]

    up_t = order(
        blocks(index, [up_t, up_x], [((dim // 2, units), BF)], side_body, name="side")[0]
    )
    up_z = over(up_t, 1)
    down_z = order(down_z)
    down = order(join(index, 2, down, down_z))
    down_z = over(down, 1)
    qk_z = over(qk, 2)
    vo_z = order(vo_z)
    vo = order(sums(index, [vo, vo_z])[0])
    for n in range(3, len(bits)):
        vo = sums(index, [vo, over(vo, n)])[0]
    vo_z = over(vo, 1)
    down_z = order(down_z)
    down = order(join(index, 1, down, down_z))
    down_x = over(down, 0)
    qk_z = order(qk_z)
    qk = order(sums(index, [qk, qk_z])[0])
    for n in range(3, len(bits)):
        qk = sums(index, [qk, over(qk, n)])[0]
    qk_x = over(qk, 0)

    def up_body(index, ins, outs):
        for ref, z in zip(ins, (index[1], 1 - index[1])):
            for h, x in enumerate((index[0], 1 - index[0])):
                outs[0][rows_at(z * (dim // 2), dim // 2), rows_at(x * half, half, LANES)] = wide(
                    ref[:, h * half : (h + 1) * half]
                )

    def down_body(index, ins, outs):
        for ref, x in zip(ins, (index[0], 1 - index[0])):
            outs[0][rows_at(x * half, half), :] = wide(ref[...])

    up_z = order(up_z)
    grad_up = blocks(index, [up_t, up_z], [((dim, units), F32)], up_body, name="up_out")[0]
    vo_z = order(vo_z)
    qk_x = order(qk_x)

    def attn_body(index, ins, outs):
        own, other = index[0], 1 - index[0]
        outs[0][rows_at(own * width, width), :] = wide(ins[0][...])
        outs[0][rows_at(other * width, width), :] = wide(ins[1][...])
        own, other = index[1], 1 - index[1]
        outs[1][own] = wide(ins[2][...])
        outs[1][other] = wide(ins[3][...])

    grad_qk, grad_vo = blocks(
        index,
        [qk, qk_x, vo, vo_z],
        [((2 * width, dim), F32), ((2, width, dim), F32)],
        attn_body,
        name="attn_out",
    )
    grad_qkv = jnp.concatenate([grad_qk, grad_vo[0]])
    grad_qkv = grad_qkv.reshape(3, width, dim).transpose(2, 0, 1)
    grad_output = grad_vo[1]
    down_x = order(down_x)
    grad_down = blocks(index, [down, down_x], [((units, dim), F32)], down_body, name="down_out")[0]

    shared = jnp.concatenate([sums_attn.reshape(-1), sums_ffn.reshape(-1)])
    owned = [jnp.concatenate([g_query[r], g_value[r], g_bias_up[r]]) for r in range(4)]
    near = jnp.concatenate([shared, owned[0], owned[2]])
    near = near + core(jnp.concatenate([shared, owned[1], owned[3]]))
    split = shared.shape[0] + owned[0].shape[0]
    total = near[:split] + over_y(jnp.concatenate([near[: shared.shape[0]], near[split:]]))
    head = shared.shape[0] + 2 * width
    total = jnp.concatenate(
        [
            total[:head],
            jnp.where(ix == 0, total[head:], jnp.roll(total[head:], half)),
        ]
    )
    for n in range(len(bits)):
        total = total + over(total, n)
    g_gain_attn, g_shift_attn, g_bias_output, g_gain_ffn, g_shift_ffn, g_bias_down = (
        total[i * dim : (i + 1) * dim] for i in range(6)
    )
    g_bias_query = total[6 * dim : 6 * dim + width]
    g_bias_value = total[6 * dim + width : 6 * dim + 2 * width]
    return (
        mixed,
        input_grad,
        grad_qkv,
        g_bias_query,
        g_bias_value,
        grad_output,
        g_bias_output,
        g_gain_attn,
        g_shift_attn,
        grad_up,
        total[head:],
        grad_down,
        g_bias_down,
        g_gain_ffn,
        g_shift_ffn,
    )


def solution(mesh):
    return jax.shard_map(
        local,
        mesh=mesh,
        in_specs=(
            P(("dp", "tensor"), None),
            P(None, None, "tensor"),
            P("tensor"),
            P("tensor"),
            P("tensor", None),
            P(),
            P(),
            P(),
            P(None, "tensor"),
            P("tensor"),
            P("tensor", None),
            P(),
            P(),
            P(),
            P(("dp", "tensor"), None),
            P(("dp", "tensor")),
            P(("dp", "tensor")),
            P("dp", None),
        ),
        out_specs=(
            P(("dp", "tensor"), None),
            P(("dp", "tensor"), None),
            P(None, None, "tensor"),
            P("tensor"),
            P("tensor"),
            P("tensor", None),
            P(),
            P(),
            P(),
            P(None, "tensor"),
            P("tensor"),
            P("tensor", None),
            P(),
            P(),
            P(),
        ),
        check_vma=False,
    )
```

```python
import functools
import math

import jax
import jax.numpy as jnp
from jax import lax
from jax.experimental import pallas as pl
from jax.experimental.pallas import tpu as pltpu
from jax.sharding import PartitionSpec as P

HEAD_DIM = 64
SPAN = 128
LANES = 128
EPSILON = 1e-12
SQRT_HALF = 0.7071067811865476
INV_ROOT_TWO_PI = 0.3989422804014327
SCALE = 1.0 / math.sqrt(HEAD_DIM)
BF = jnp.bfloat16
F32 = jnp.float32
MIB = 1 << 20

CORE, Y = 1, 2


def nn(a, b):
    return lax.dot_general(a, b, (((1,), (0,)), ((), ())), preferred_element_type=F32)


def nt(a, b):
    return lax.dot_general(a, b, (((1,), (1,)), ((), ())), preferred_element_type=F32)


def tn(a, b):
    return lax.dot_general(a, b, (((0,), (0,)), ((), ())), preferred_element_type=F32)


SCALARS = pl.BlockSpec(memory_space=pltpu.SMEM)
WHOLE = pl.BlockSpec(memory_space=pltpu.VMEM)
LEFT = pl.BlockSpec(memory_space=pl.ANY)
FAR = pl.BlockSpec(memory_space=pltpu.HBM)


def call(body, index, args, out, scratch=(), vmem=24, left=(), far=(), cold=(), name=None):
    count = len(args)
    fetched = list(far)
    args = [
        pltpu.with_memory_space_constraint(t, pltpu.HBM) if i in fetched else t
        for i, t in enumerate(args)
    ]
    cold = list(cold)

    def run(index, *refs):
        refs = list(refs)
        places = refs[count + len(out) :]
        refs, places = refs[: count + len(out)], places
        ins, places = places[: len(fetched)], places[len(fetched) :]
        outs, places = places[: len(cold)], places[len(cold) :]
        sems, rest = places[0], places[1:]
        io = Transfers()
        for j, (i, place) in enumerate(zip(fetched, ins)):
            io.coming.append((place, pltpu.make_async_copy(refs[i], place, sems.at[j])))
            refs[i] = place
        for j, (i, place) in enumerate(zip(cold, outs)):
            copy = pltpu.make_async_copy(place, refs[count + i], sems.at[len(fetched) + j])
            io.going.append((place, copy))
            refs[count + i] = place
        for _, copy in io.coming:
            copy.start()
        body(io, index, *refs, *rest)
        assert not io.coming, name
        io.push(*outs)
        for copy in io.gone:
            copy.wait()

    places = [pltpu.HBM if i in cold else None for i in range(len(out))]
    return pl.pallas_call(
        run,
        out_shape=[
            jax.ShapeDtypeStruct(s, t) if place is None else place(s, t)
            for (s, t), place in zip(out, places)
        ],
        in_specs=[SCALARS]
        + [FAR if i in fetched else LEFT if i in left else WHOLE for i in range(count)],
        out_specs=[WHOLE if place is None else FAR for place in places],
        scratch_shapes=[pltpu.VMEM(args[i].shape, args[i].dtype) for i in fetched]
        + [pltpu.VMEM(*out[i]) for i in cold]
        + [pltpu.SemaphoreType.DMA((max(len(fetched) + len(cold), 1),))]
        + list(scratch),
        compiler_params=pltpu.CompilerParams(vmem_limit_bytes=vmem * MIB),
        cost_estimate=pl.CostEstimate(flops=1000, bytes_accessed=0, transcendentals=0),
        name=name,
    )(index, *args)


class Transfers:
    def __init__(self):
        self.coming, self.going, self.gone = [], [], []

    def need(self, *refs):
        for place, copy in list(self.coming):
            if any(place is ref for ref in refs):
                copy.wait()
                self.coming = [t for t in self.coming if t[0] is not place]

    def push(self, *refs):
        for place, copy in list(self.going):
            if any(place is ref for ref in refs):
                copy.start()
                self.gone.append(copy)
                self.going = [t for t in self.going if t[0] is not place]


def rows_at(start, size, unit=16):
    return pl.ds(pl.multiple_of(start, unit), size)


def gather_weights(index, halves, w, sems):
    width = w.shape[0] // 8
    pair = 2 * width
    copies = []
    for block in range(2):
        for order in range(2):
            which = index[0] if order == 0 else 1 - index[0]
            for j in range(2):
                start = (2 * which + j) * pair + block * width
                copies.append(
                    pltpu.make_async_copy(
                        halves[2 * block + order].at[pl.ds(j * width, width)],
                        w.at[rows_at(start, width)],
                        sems.at[len(copies)],
                    )
                )
    for copy in copies:
        copy.start()
    return copies


def probs_of(scores):
    expo = jnp.exp(scores - jnp.max(scores, axis=0, keepdims=True))
    return expo * (1.0 / jnp.sum(expo, axis=0, keepdims=True))


def two_heads(value):
    low = lax.broadcasted_iota(jnp.int32, value.shape, 1) < HEAD_DIM
    zero = jnp.zeros_like(value)
    return jnp.concatenate([jnp.where(low, value, zero), jnp.where(low, zero, value)], axis=0)


def of_two_heads(value):
    half = value.shape[0] // 2
    low = lax.broadcasted_iota(jnp.int32, (half, value.shape[1]), 1) < HEAD_DIM
    return jnp.where(low, value[:half], value[half:])


def norm_rows(summed):
    centre = summed - jnp.mean(summed, axis=-1, keepdims=True)
    factor = lax.rsqrt(jnp.mean(centre * centre, axis=-1, keepdims=True) + EPSILON)
    return centre * factor, factor


def norm_back(incoming, normed, factor, gain):
    scaled = incoming * gain
    return factor * (
        scaled
        - jnp.mean(scaled, axis=-1, keepdims=True)
        - normed * jnp.mean(scaled * normed, axis=-1, keepdims=True)
    )


def attend_body(last, io, index, x, w0a, w0b, w1a, w1b, bias, bias_col, acc, *rest):
    if last:
        norms, q, k, v, ctx, w, acc_out, second, first_low, first_turned, vt, sems = rest
    else:
        q, k, v, ctx, w, acc_out, vt, sems = rest
    rows = x.shape[0]
    pair = bias.shape[1]
    copies = gather_weights(index, (w0a, w0b, w1a, w1b), w, sems)
    for copy in copies:
        copy.wait()
    query = (nt(x[...], w[:pair, :]) + bias[0:1, :]).astype(BF)
    q[...] = (query.astype(F32) * SCALE).astype(BF)
    k[...] = nt(x[...], w[pair : 2 * pair, :]).astype(BF)
    v[...] = (nt(x[...], w[2 * pair : 3 * pair, :]) + bias[1:2, :]).astype(BF)
    vt[...] = (nt(w[2 * pair : 3 * pair, :], x[...]) + bias_col[...]).astype(BF)

    def span(i, _):
        here = rows_at(i * SPAN, SPAN, SPAN)
        for tile in range(pair // LANES):
            cut = slice(tile * LANES, (tile + 1) * LANES)
            scores = nt(two_heads(k[here, cut]), q[here, cut])
            for h in range(2):
                probs = probs_of(scores[h * SPAN : (h + 1) * SPAN])
                own = slice(tile * LANES + h * HEAD_DIM, tile * LANES + (h + 1) * HEAD_DIM)
                ctx[own, here] = nn(vt[own, here], probs.astype(BF)).astype(BF)
        return 0

    io.push(q, k, v, w)
    lax.fori_loop(0, rows // SPAN, span, 0)
    io.push(ctx)
    total = acc[...] + tn(ctx[...], w[3 * pair :, :])
    acc_out[...] = total
    if last:
        normed, _ = norm_rows(total)
        first = normed * norms[0:1, :] + norms[1:2, :]
        low = first.astype(BF)
        first_low[...] = low
        first_turned[...] = low.T
        second[...] = first + norms[2:3, :]


def attend(index, x, halves, bias, bias_col, acc, norms=None):
    rows, dim = x.shape
    pair = bias.shape[1]
    last = norms is not None
    args = [x, *halves, bias, bias_col, acc] + ([norms] if last else [])
    out = [((rows, pair), BF)] * 3 + [((pair, rows), BF), ((4 * pair, dim), BF), ((rows, dim), F32)]
    if last:
        out += [((rows, dim), F32), ((rows, dim), BF), ((dim, rows), BF)]
    return call(
        functools.partial(attend_body, last),
        index,
        args,
        out,
        [pltpu.VMEM((pair, rows), BF), pltpu.SemaphoreType.DMA((8,))],
        left=(1, 2, 3, 4),
        cold=range(5),
        name="attend",
    )


SMALL = 16


def put_small(message, at, value):
    high = value.astype(BF)
    message[at : at + SMALL, :] = high
    message[at + SMALL : at + 2 * SMALL, :] = (value - high.astype(F32)).astype(BF)


def get_small(message, at):
    return message[at : at + SMALL, :].astype(F32) + message[at + SMALL : at + 2 * SMALL, :].astype(F32)


def attend_back_body(last, io, index, ctx, grad, w, x, q, k, v, acc, *rest):
    if last:
        small0, small1, *rest = rest
    own, *messages, sums, acc_out, kt, dc, dqt, dk, dv = rest
    rows = x.shape[0]
    pair = ctx.shape[0]
    width = pair // 2

    def put(part, value):
        value = value.astype(BF)
        own[part] = value[:width]
        per = 4 // len(messages)
        start = part % per * width
        messages[part // per][start : start + width, :] = value[width:]

    io.need(ctx, grad)
    put(3, nn(ctx[...], grad[...]))
    io.need(w, x)
    kt[...] = nt(w[pair : 2 * pair, :], x[...]).astype(BF)
    dc[...] = nt(grad[...], w[3 * pair :, :]).astype(BF)
    io.need(q, k, v)

    def span(i, _):
        here = rows_at(i * SPAN, SPAN, SPAN)
        for tile in range(pair // LANES):
            cut = slice(tile * LANES, (tile + 1) * LANES)
            query, grads = q[here, cut], dc[here, cut]
            scores = nt(two_heads(k[here, cut]), query)
            d_probs = nt(two_heads(v[here, cut]), grads)
            low_probs, low_scores = [], []
            for h in range(2):
                own_rows = slice(h * SPAN, (h + 1) * SPAN)
                probs = probs_of(scores[own_rows])
                inner = jnp.sum(d_probs[own_rows] * probs, axis=0, keepdims=True)
                d_scores = (probs * (d_probs[own_rows] - inner)).astype(BF)
                low_probs.append(probs.astype(BF))
                low_scores.append(d_scores)
                mine = slice(tile * LANES + h * HEAD_DIM, tile * LANES + (h + 1) * HEAD_DIM)
                dqt[mine, here] = (nn(kt[mine, here], d_scores) * SCALE).astype(BF)
            dk[here, cut] = of_two_heads(nn(jnp.concatenate(low_scores, axis=0), query)).astype(BF)
            dv[here, cut] = of_two_heads(nn(jnp.concatenate(low_probs, axis=0), grads)).astype(BF)
        return 0

    lax.fori_loop(0, rows // SPAN, span, 0)
    put(0, nn(dqt[...], x[...]))
    put(1, tn(dk[...], x[...]))
    put(2, tn(dv[...], x[...]))
    ones = jnp.ones((8, rows), BF)
    sum_q, sum_v = nt(ones, dqt[...])[0:1], nn(ones, dv[...])[0:1]
    for block in range(2):
        cut = slice(block * width, (block + 1) * width)
        sums[block : block + 1, 0:width] = sum_q[:, cut]
        sums[block : block + 1, width : 2 * width] = sum_v[:, cut]
    if last:
        for block, small in enumerate((small0, small1)):
            small[6:7, 0:pair] = sums[block : block + 1, :]
        put_small(messages[0], 2 * width, small1[...])
    acc_out[...] = (
        acc[...]
        + tn(dqt[...], w[:pair, :])
        + nn(dk[...], w[pair : 2 * pair, :])
        + nn(dv[...], w[2 * pair : 3 * pair, :])
    )


def attend_back(index, kept, grad, x, acc, small=()):
    rows, dim = x.shape
    pair = kept[3].shape[0]
    width = pair // 2
    last = bool(small)

    def body(io, index, *refs):
        if not last:
            return attend_back_body(False, io, index, *refs)
        ins, (sums_attn, sums_ffn, sums_far), ups, rest = refs[:8], refs[8:11], refs[11:15], refs[15:]
        outs, out0, spare, scratch = rest[:5], rest[5], rest[6], rest[7:]
        for block, out in enumerate((out0, spare)):
            out[...] = jnp.zeros_like(out)
            out[0:3, :] = sums_attn[...]
            out[3:6, :] = sums_ffn[...]
            out[7:8, :] = ups[block][0:1, :]
            out[8:9, 0:pair] = sums_far[block : block + 1, :]
            out[9:10, :] = ups[2 + block][0:1, :]
        return attend_back_body(True, io, index, *ins, out0, spare, *outs, *scratch)

    out = [((4, width, dim), BF)]
    out += [((pair + 2 * SMALL, dim), BF), ((pair, dim), BF)] if last else [((2 * pair, dim), BF)]
    out += [((2, pair), F32), ((rows, dim), F32)]
    out += [((SMALL, dim), F32)] if last else []
    return call(
        body,
        index,
        [kept[3], grad, kept[4], x, *kept[:3], acc, *small],
        out,
        ([pltpu.VMEM((SMALL, dim), F32)] if last else [])
        + [pltpu.VMEM((pair, rows), BF), pltpu.VMEM((rows, pair), BF)]
        + [pltpu.VMEM((pair, rows), BF)]
        + [pltpu.VMEM((rows, pair), BF), pltpu.VMEM((rows, pair), BF)],
        far=(0, 2, 4, 5, 6),
        name="attend_back",
    )


def gelu_parts(upper):
    phi = 0.5 * (1.0 + lax.erf(upper * SQRT_HALF))
    slope = phi + upper * jnp.exp(-0.5 * upper * upper) * INV_ROOT_TWO_PI
    return (upper * phi).astype(BF), slope.astype(BF)


def feed_body(count, io, index, first, *refs):
    weights, acc, bias = refs[: 2 * count], refs[2 * count], refs[2 * count + 1 : 3 * count + 1]
    refs = refs[3 * count + 1 :]
    active, slope, acc_out = refs[:count], refs[count : 2 * count], refs[2 * count]
    total = None
    for i in range(count):
        up, down = weights[2 * i : 2 * i + 2]
        size = up.shape[1]
        step = min(size, 384)
        for at in range(0, size, step):
            cut = slice(at, at + step)
            act, slp = gelu_parts(nn(first[...], up[:, cut]) + bias[i][:, cut])
            active[i][cut, :] = act.T
            slope[i][:, cut] = slp
            more = nn(act, down[cut, :])
            total = more if total is None else total + more
        io.push(active[i], slope[i])
    acc_out[...] = total + acc[...]


def feed(index, first, acc, bias, up, down):
    rows, dim = first.shape
    count, size = len(up), up[0].shape[1]
    out = call(
        functools.partial(feed_body, count),
        index,
        [first, *(t for both in zip(up, down) for t in both), acc, *bias],
        [((size, rows), BF)] * count + [((rows, size), BF)] * count + [((rows, dim), F32)],
        name="feed",
    )
    return out[:count], out[count : 2 * count], out[2 * count]


def x_half(index, h, size):
    return rows_at((index[0] if h == 0 else 1 - index[0]) * size, size, LANES)


def feed_up_body(io, index, first, *refs):
    up, bias, plain, active, slope = refs[:2], refs[2], refs[3:5], refs[5:7], refs[7:9]
    for h in range(2):
        there = x_half(index, h, up[h].shape[1])
        act, slp = gelu_parts(nn(first[...], up[h][...]) + bias[:, there])
        plain[h][...] = act
        active[h][...] = act.T
        slope[h][...] = slp


def feed_up(index, first, bias, up):
    rows, dim = first.shape
    size = up[0].shape[1]
    out = call(
        feed_up_body,
        index,
        [first, *up, bias],
        [((rows, size), BF)] * 2 + [((size, rows), BF)] * 2 + [((rows, size), BF)] * 2,
        name="feed_up",
    )
    return out[:2], out[2:4], out[4:]


def down_dot(index, active, down):
    size = active[0].shape[1]
    first, second = (nn(active[h][...], down[x_half(index, h, size), :]) for h in range(2))
    return first + second


def feed_down(index, acc, active, down):
    def body(io, index, acc, first, second, down, out):
        out[...] = acc[...] + down_dot(index, (first, second), down)

    return call(body, index, [acc, *active, down], [(acc.shape, F32)], name="feed_down")[0]


def down_back_body(near, more, last, io, index, grad, *refs):
    count = 1 if near else 2
    active, refs = refs[:count], refs[count:]
    other, refs = (refs[0], refs[1:]) if more else (None, refs)
    far, refs = (refs[0], refs[1:]) if last else (None, refs)
    out, refs = refs[0], refs[1:]
    half = (out if last else out.at[0]).shape[0]
    if last:
        send, sems = refs
        copy = pltpu.make_async_copy(far.at[1], send.at[0], sems.at[0])
        copy.start()
    for h in range(2):
        if near:
            start = (index[0] if h == 0 else 1 - index[0]) * half
            value = nn(active[0][rows_at(start, half, LANES), :], grad[...])
        else:
            value = nn(active[h][...], grad[...])
        if more:
            value = value + other[h].astype(F32)
        if last and h == 0:
            out[...] = value.astype(BF)
        elif last:
            send[1] = value.astype(BF)
        else:
            out[h] = value.astype(BF)
    if last:
        copy.wait()


def down_back(index, grad, active, other=None, far=None):
    rows, dim = grad.shape
    near = len(active) == 1
    units = sum(t.shape[0] for t in active)
    more, last = other is not None, far is not None
    parts = (2, units // 2, dim)
    args = [grad, *active] + ([other] if more else []) + ([far] if last else [])
    return call(
        functools.partial(down_back_body, near, more, last),
        index,
        args,
        [((units // 2, dim), BF), (parts, BF)] if last else [(parts, BF)],
        [pltpu.SemaphoreType.DMA((1,))] if last else [],
        left=[len(args) - 1] if last else [],
        name="down_back",
    )


def up_back_body(near, more, apart, io, index, grad, *refs):
    count = 1 if near else 2
    down, slope, refs = refs[0], refs[1 : 1 + count], refs[1 + count :]
    first_turned, up, refs = refs[0], refs[1 : 1 + count], refs[1 + count :]
    other, refs = (refs[:2], refs[2:]) if more else ((), refs)
    acc, refs = refs[0], refs[1:]
    g_up, refs = (refs[:2], refs[2:]) if apart else ((refs[0].at[0], refs[0].at[1]), refs[1:])
    sums, acc_out = refs
    half = sums.shape[1] // 2
    size = first_turned.shape[0] // 2
    ones = jnp.ones((8, grad.shape[0]), BF)
    total = acc[...]
    for h in range(2):
        there = x_half(index, h, half)
        cut = slice(h * half, (h + 1) * half)
        slp = wide(slope[0][:, there] if near else slope[h][...])
        d_upper = (nt(grad[...], down[there, :]) * slp).astype(BF)
        sums[:, there] = nn(ones, d_upper)
        for z in range(2):
            rows = rows_at((index[1] if z == 0 else 1 - index[1]) * size, size, LANES)
            value = nn(first_turned[rows, :], d_upper)
            if more:
                value = value + other[z][:, cut].astype(F32)
            g_up[z][:, cut] = value.astype(BF)
        total = total + nt(d_upper, up[0][:, there] if near else up[h][...])
    acc_out[...] = total


def up_back(index, first_turned, grad, acc, slope, up, down, other=(), apart=False):
    rows, dim = grad.shape
    near = len(up) == 1
    units = down.shape[0]
    half = (dim // 2, units)
    *got, sums, total = call(
        functools.partial(up_back_body, near, bool(other), apart),
        index,
        [grad, down, *slope, first_turned, *up, *other, acc],
        ([(half, BF)] * 2 if apart else [((2, *half), BF)])
        + [((8, units), F32), ((rows, dim), F32)],
        name="up_back",
    )
    return got, sums, total


def pack_body(io, index, qkv, output, biases, first, second):
    half = second.shape[0]
    rest = qkv.shape[0] - half
    for x, low, high in ((0, first, second), (1, second, first)):

        @pl.when(index[0] == x)
        def _():
            low[:half, :] = qkv[:half, :]
            high[:rest, :] = qkv[half:, :]
            high[rest:half, :] = output[...]

    first[half:, :] = biases[...]


def pack(index, qkv, output, biases):
    rows = qkv.shape[0] + output.shape[0]
    dim = output.shape[1]
    out = [((rows // 2 + biases.shape[0], dim), BF), ((rows // 2, dim), BF)]
    return tuple(call(pack_body, index, [qkv, output, biases], out, name="pack"))


def turn_body(io, index, first, second, down, acc, out_grad, cls_rows, norms, *refs):
    mixed, d_second, low, sums = refs
    second = acc[...] + down_dot(index, (first, second), down)
    normed, factor = norm_rows(second)
    mixed[...] = (normed * norms[0:1, :] + norms[1:2, :]).astype(BF)
    spans = cls_rows.shape[0]
    shape = (spans, SPAN, out_grad.shape[1])
    first_row = lax.broadcasted_iota(jnp.int32, shape, 1) == 0
    incoming = wide(out_grad[...]).reshape(shape)
    incoming = incoming + jnp.where(first_row, cls_rows[...][:, None, :], 0.0)
    incoming = incoming.reshape(out_grad.shape)
    grad = norm_back(incoming, normed, factor, norms[0:1, :])
    d_second[...] = grad
    low[...] = grad.astype(BF)
    sums[0:1, :] = jnp.sum(incoming * normed, axis=0, keepdims=True)
    sums[1:2, :] = jnp.sum(incoming, axis=0, keepdims=True)
    sums[2:3, :] = jnp.sum(grad.astype(BF).astype(F32), axis=0, keepdims=True)


def turn(index, acc, cotangent, norms, active, down):
    size = acc.shape
    return call(
        turn_body,
        index,
        [*active, down, acc, *cotangent, norms],
        [(size, BF), (size, F32), (size, BF), ((3, size[1]), F32)],
        name="turn",
    )


def first_back_body(io, index, attended, incoming, norms, d_attn, low, sums):
    normed, factor = norm_rows(attended[...])
    grad = norm_back(incoming[...], normed, factor, norms[0:1, :])
    d_attn[...] = grad
    low[...] = grad.astype(BF)
    sums[0:1, :] = jnp.sum(incoming[...] * normed, axis=0, keepdims=True)
    sums[1:2, :] = jnp.sum(incoming[...], axis=0, keepdims=True)
    sums[2:3, :] = jnp.sum(grad.astype(BF).astype(F32), axis=0, keepdims=True)


def first_back(index, attended, incoming, norms):
    size = attended.shape
    return call(
        first_back_body,
        index,
        [attended, incoming, norms],
        [(size, F32), (size, BF), ((3, size[1]), F32)],
        name="first_back",
    )


def wide(value):
    return value.astype(F32)


def blocks(index, args, out, body, name="blocks"):
    def run(io, index, *refs):
        body(index, refs[: len(args)], refs[len(args) :])

    return call(run, index, args, out, name=name)


def sums(index, *groups):
    def body(_, ins, outs):
        at = 0
        for group, out in zip(groups, outs):
            total = wide(ins[at][...])
            for i in range(1, len(group)):
                total = total + wide(ins[at + i][...])
            out[...] = total.astype(BF)
            at += len(group)

    return blocks(
        index,
        [a for group in groups for a in group],
        [(group[0].shape, BF) for group in groups],
        body,
        name="sums",
    )


def split_sum(index, which, a, b):
    half = a.shape[0] // 2

    def body(index, ins, outs):
        for out, bit in zip(outs, (index[which], 1 - index[which])):
            there = rows_at(bit * half, half)
            out[...] = (wide(ins[0][there, :]) + wide(ins[1][there, :])).astype(BF)

    return blocks(index, [a, b], [((half, a.shape[1]), BF)] * 2, body, name="split_sum")


def join(index, which, own, other):
    half = own.shape[0]

    def body(index, ins, outs):
        for value, bit in zip(ins, (index[which], 1 - index[which])):
            outs[0][rows_at(bit * half, half), :] = value[...]

    return blocks(index, [own, other], [((2 * half, own.shape[1]), BF)], body, name="join")[0]


def swap(value, axis, bit):
    size = lax.axis_size(axis)
    return lax.ppermute(value, axis, [(i, i ^ bit) for i in range(size)])


class Order:
    def __init__(self, token):
        self.token = token

    def __call__(self, *values):
        self.token, *values = lax.optimization_barrier((self.token, *values))
        return values[0] if len(values) == 1 else values


def pick_half(value, index, axis=0):
    half = value.shape[axis] // 2
    return lax.dynamic_slice_in_dim(value, index * half, half, axis)


def local(
    inputs,
    w_qkv,
    bias_query,
    bias_value,
    w_output,
    bias_output,
    gain_attn,
    shift_attn,
    w_up,
    bias_up,
    w_down,
    bias_down,
    gain_ffn,
    shift_ffn,
    out_grad,
    mlm_mask,
    span_doc,
    cls_grad,
):
    rows, dim = inputs.shape
    width = w_qkv.shape[2]
    units = w_up.shape[1]
    half = units // 2
    dp = lax.axis_index("dp")
    bits = [1 << i for i in range(lax.axis_size("dp").bit_length() - 1)]
    ix = dp % 2
    index = jnp.stack([ix, (dp // bits[1]) % 2, (dp // bits[2]) % 2]).astype(jnp.int32)
    order = Order(bias_output)

    def core(value):
        return swap(value, "tensor", CORE)

    def over_y(value):
        return swap(value, "tensor", Y)

    def over(value, n):
        return swap(value, "dp", bits[n])

    biases = jnp.stack([jnp.concatenate([bias_query, bias_value, bias_up[: dim - 2 * width]]), bias_up])
    parts = []
    for _ in range(3):
        parts.append(lax.reduce_precision(biases, 8, 7))
        biases = biases - parts[-1]
    biases = jnp.concatenate([*parts, jnp.zeros((SMALL - 6, dim), F32)]).astype(BF)
    attn = {0: pack(index, w_qkv.transpose(1, 2, 0).reshape(3 * width, dim), w_output, biases)}
    attn_a = over_y(attn[0][0])
    attn[1] = tuple(core(t) for t in attn[0])
    up_a = over_y(pick_half(w_up, ix, 1))

    def biases_of(halves):
        rows_here = halves[0][2 * width :].astype(F32)
        return rows_here[0:2] + rows_here[2:4] + rows_here[4:6]

    def attend_biases(*small):
        pairs = [
            jnp.concatenate([t[0, at : at + width] for t in small]) for at in (0, width)
        ]
        return jnp.stack(pairs), pairs[1][:, None]

    norms_attn = jnp.stack([gain_attn, shift_attn, bias_down])
    norms_ffn = jnp.stack([gain_ffn, shift_ffn])
    kept = {}
    attended = bias_output + inputs.astype(F32)
    small = {0: jnp.stack([jnp.concatenate([bias_query, bias_value, bias_up[: dim - 2 * width]]), bias_up])}

    weighting = jnp.where(mlm_mask == 1, 2.0, 0.5).astype(BF)
    docs_here = cls_grad.shape[0]
    local_doc = span_doc - dp * docs_here
    picker = (local_doc[:, None] == jnp.arange(docs_here, dtype=jnp.int32)[None, :]).astype(F32)
    cls_rows = jnp.dot(picker, cls_grad.astype(F32), precision=lax.Precision.HIGHEST)
    cotangent = [out_grad * weighting[:, None], cls_rows]

    near = order(*attn[0], *attn[1], attended)
    attn[0], attn[1], attended = tuple(near[:2]), tuple(near[2:4]), near[4]
    small[1] = biases_of(attn[1])
    *kept[0], attended = attend(
        index, inputs, attn[0] + attn[1], *attend_biases(small[0], small[1]), attended
    )

    attended, attn_a, w_up, w_down, *cotangent = order(
        attended, attn_a, w_up, w_down, *cotangent
    )
    attn_b = over(attn_a, 0)
    far_a = core(attn_a)
    up, down = {0: w_up}, {0: w_down}
    down[2] = over_y(w_down)
    up[1], down[1] = core(w_up), core(w_down)
    up_a = order(up_a)
    up_b = over(up_a, 0)
    up_far_a = core(up_a)
    attn_b, far_a = order(attn_b, far_a)
    far_b = order(core(attn_b))
    attn[2], attn[3] = (attn_a, attn_b), (far_a, far_b)
    small[2], small[3] = biases_of(attn[2]), biases_of(attn[3])
    *kept[2], attended, second, first_low, first_turned = attend(
        index,
        inputs,
        attn[2] + attn[3],
        *attend_biases(small[2], small[3]),
        attended,
        norms_attn,
    )

    first_low, up[1], down[1] = order(first_low, up[1], down[1])
    act_near, slope_near, second = feed(
        index, first_low, second, [small[r][1:2] for r in (0, 1)], [up[0], up[1]], [down[0], down[1]]
    )
    second, up_b, up_far_a = order(second, up_b, up_far_a)
    up_far_b = core(up_b)
    plain_2, act_2, slope_2 = feed_up(index, first_low, small[2][1:2], [up_a, up_b])
    *plain_2, down[2] = order(*plain_2, down[2])
    down[3] = core(down[2])
    second, up_far_b = order(feed_down(index, second, plain_2, down[2]), up_far_b)
    plain_3, act_3, slope_3 = feed_up(index, first_low, small[3][1:2], [up_far_a, up_far_b])
    *plain_3, down[3] = order(*plain_3, down[3])
    mixed, d_second, branch_grad, sums_ffn = turn(
        index, second, cotangent, norms_ffn, plain_3, down[3]
    )

    g_bias_up = {}
    act_of = [[act_near[0]], [act_near[1]], act_2, act_3]
    slope_of = [[slope_near[0]], [slope_near[1]], slope_2, slope_3]
    up_of = [[up[0]], [up[1]], [up_a, up_b], [up_far_a, up_far_b]]

    def back_up(r, total, other=(), apart=False):
        got, g_bias_up[r], total = up_back(
            index, first_turned, branch_grad, total, slope_of[r], up_of[r], down[r], other, apart
        )
        return order(*got, total)

    down_3 = core(order(*down_back(index, branch_grad, act_of[3])))
    down_1 = core(order(*down_back(index, branch_grad, act_of[1])))
    *up_3, d_first = back_up(3, d_second, apart=True)
    up_3 = [core(t) for t in up_3]
    down_3 = order(down_3)
    far_down = order(*down_back(index, branch_grad, act_of[2], down_3))
    down_1 = order(down_1)
    near_down, down_send = order(*down_back(index, branch_grad, act_of[0], down_1, far_down))
    down_x = over(down_send, 0)
    *up_1, d_first = back_up(1, order(d_first), apart=True)
    up_3 = order(*up_3)
    up_1 = [core(t) for t in up_1]
    far_up, d_first = back_up(2, d_first, up_3)
    up_y = over_y(far_up)
    up_1 = order(*up_1)
    near_up, d_first = back_up(0, d_first, up_1)

    d_attn, attended_grad, sums_attn = first_back(index, attended, d_first, norms_attn)

    def attention_back(r, total, small=()):
        return order(
            *attend_back(
                index, kept[r], attended_grad, inputs, total, small
            )
        )

    far_attn, message, sums_far, input_grad = attention_back(2, d_attn)

    def add(*values):
        total = wide(values[0])
        for value in values[1:]:
            total = total + wide(value)
        return total.astype(BF)

    def more(value):
        for n in range(3, len(bits)):
            value = sums(index, [value, over(value, n)])[0]
        return value

    def run(name, args, out, body):
        dtypes = [(t[:-1], F32) if t[-1] == F32 else (t, BF) for t in out]
        return order(*blocks(index, args, dtypes, body, name=name))

    def both(index, n):
        return index[n], 1 - index[n]

    part = width // 2
    extra = 2 * SMALL

    def down_1(index, ins, outs):
        far, near, came = ins
        size = half // 2
        for i, bit in enumerate(both(index, 1)):
            there = rows_at(bit * size, size)
            for j, mine in enumerate((far.at[0], near)):
                place = outs[j] if i == 0 else outs[2].at[j]
                place[...] = add(mine[there, :], came[j, there, :])

    quarter = (half // 2, dim)
    down_x, input_grad, message = order(down_x, input_grad, message)
    from_core = core(message)
    down_f, down_n, down_s = run(
        "down_1", [far_down, near_down, down_x], [quarter, quarter, (2, *quarter)], down_1
    )
    down_z = over(down_s, 1)
    input_grad = order(input_grad)

    near_attn, *to_core, _, input_grad, little = attention_back(
        0, input_grad, (sums_attn, sums_ffn, sums_far, *(g_bias_up[r] for r in range(4)))
    )
    to_core = [core(t) for t in to_core]

    def up_1(_, ins, outs):
        for i in range(2):
            outs[i][...] = add(ins[0][i], ins[1][i])

    from_core, up_y = order(from_core, up_y)
    up_k, up_s = run("up_1", [near_up, up_y], [(dim // 2, units)] * 2, up_1)
    up_z = over(up_s, 1)

    def down_2(_, ins, outs):
        for i in range(2):
            outs[i][...] = add(ins[i][...], ins[2][i])

    down_z = order(down_z)
    down_f, down_n = run("down_2", [down_f, down_n, down_z], [quarter] * 2, down_2)
    down_y = over_y(down_f)

    def rows_of(part):
        return slice(part * width, (part + 1) * width)

    def qk_1(index, ins, outs):
        far, near, far_came, near_came, little = ins
        for i, bit in enumerate(both(index, 0)):
            for j, (mine, came) in enumerate(((far, far_came), (near, near_came))):
                for k in range(2):

                    @pl.when(bit == k)
                    def _():
                        value = add(mine[k], came[rows_of(k), :])
                        if i == 0:
                            outs[j][...] = value
                        else:
                            outs[2][rows_of(j), :] = value

        total = little[...] + get_small(near_came, 2 * width)
        outs[3][...] = total
        put_small(outs[2], 2 * width, total)

    rows_small = (SMALL, dim, F32)
    to_core[0] = order(to_core[0])
    qk_f, qk_n, qk_s, little = run(
        "qk_1",
        [far_attn, near_attn, from_core, to_core[0], little],
        [(width, dim), (width, dim), (2 * width + extra, dim), rows_small],
        qk_1,
    )
    qk_x = over(qk_s, 0)

    def vo_1(_, ins, outs):
        far, near, far_came, near_came = ins
        for k in range(2):
            outs[0][rows_of(k), :] = add(far[2 + k], far_came[rows_of(2 + k), :])
            outs[1][rows_of(k), :] = add(near[2 + k], near_came[rows_of(k), :])

    to_core[1] = order(to_core[1])
    vo_f, vo_n = run(
        "vo_1", [far_attn, near_attn, from_core, to_core[1]], [(2 * width, dim)] * 2, vo_1
    )

    down_y = order(down_y)
    down, vo_f = order(*sums(index, [down_n, down_y]), vo_f)
    down_z = over(down, 2)
    vo_y = over_y(vo_f)

    def up_2(_, ins, outs):
        for out, cut in zip(outs, (slice(0, half), slice(half, None))):
            out[...] = add(ins[0][:, cut], ins[1][:, cut])

    up_z = order(up_z)
    up_k, up_s = run("up_2", [up_k, up_z], [(dim // 2, half)] * 2, up_2)
    up_x = over(up_s, 0)

    def qk_2(index, ins, outs):
        far, near, came, little = ins
        for i, bit in enumerate(both(index, 1)):
            there = rows_at(bit * part, part)
            for j, mine in enumerate((far, near)):
                value = add(mine[there, :], came[rows_at(j * width + bit * part, part), :])
                if i == 0:
                    outs[j][...] = value
                else:
                    outs[2][j * part : (j + 1) * part, :] = value
        total = little[...] + get_small(came, 2 * width)
        outs[3][...] = total
        put_small(outs[2], 2 * part, total)

    qk_x = order(qk_x)
    qk_f, qk_n, qk_s, little = run(
        "qk_2",
        [qk_f, qk_n, qk_x, little],
        [(part, dim), (part, dim), (2 * part + extra, dim), rows_small],
        qk_2,
    )
    qk_z = over(qk_s, 1)

    up_x = order(up_x)
    up_t = order(*sums(index, [up_k, up_x]))
    up_z = over(up_t, 2)

    vo_y = order(vo_y)
    vo_k, vo_s = order(*split_sum(index, 0, vo_n, vo_y))
    vo_x = over(vo_s, 0)

    def qk_3(_, ins, outs):
        far, near, came, little = ins
        outs[0][:part, :] = add(far[...], came[:part, :])
        outs[1][...] = add(near[...], came[part : 2 * part, :])
        total = little[...] + get_small(came, 2 * part)
        outs[2][...] = total
        outs[3][...] = jnp.zeros_like(total)
        outs[3][0:6, :] = total[0:6]
        outs[3][6:8, :] = total[8:10]
        put_small(outs[0], part, outs[3][...])

    qk_z = order(qk_z)
    qk_f, qk_n, little, _ = run(
        "qk_3",
        [qk_f, qk_n, qk_z, little],
        [(part + extra, dim), (part, dim), rows_small, rows_small],
        qk_3,
    )
    qk_y = over_y(qk_f)

    down_z = order(down_z)
    down = order(more(*sums(index, [down, down_z])))
    down_z = over(down, 1)

    def qk_4(_, ins, outs):
        mine, came, little = ins
        outs[0][:part, :] = add(mine[...], came[:part, :])
        total = little[...] + get_small(came, part)
        outs[1][...] = total
        put_small(outs[0], part, total)

    qk_y = order(qk_y)
    qk, little = run("qk_4", [qk_n, qk_y, little], [(part + extra, dim), rows_small], qk_4)
    qk_z = over(qk, 2)

    vo_x = order(vo_x)
    vo = order(*sums(index, [vo_k, vo_x]))
    vo_z = over(vo, 1)

    up_z = order(up_z)
    up_t = order(more(*sums(index, [up_t, up_z])))
    up_x = over(up_t, 0)

    down_z = order(down_z)
    down = order(join(index, 1, down, down_z))
    down_x = over(down, 0)

    def qk_5(_, ins, outs):
        mine, came, little = ins
        outs[0][...] = add(mine[:part, :], came[:part, :])
        outs[1][...] = little[...] + get_small(came, part)

    qk_z = order(qk_z)
    qk, little = run("qk_5", [qk, qk_z, little], [(part, dim), rows_small], qk_5)
    qk = more(qk)
    for n in range(3, len(bits)):
        little = little + over(little, n)
    qk_z = over(qk, 1)

    vo_z = order(vo_z)
    vo = order(*sums(index, [vo, vo_z]))
    vo_z = over(vo, 2)

    def up_5(_, ins, outs):
        for i in range(2):
            outs[0][:, i * half : (i + 1) * half] = ins[i][...]

    up_x = order(up_x)
    up_t = run("up_5", [up_t, up_x], [(dim // 2, units)], up_5)
    up_z = over(up_t, 1)

    qk_z = order(qk_z)
    qk = order(join(index, 1, qk, qk_z))
    qk_x = over(qk, 0)

    def up_out(index, ins, outs):
        for ref, z in zip(ins, both(index, 1)):
            rows_here = rows_at(z * (dim // 2), dim // 2)
            for h, x in enumerate(both(index, 0)):
                outs[0][rows_here, rows_at(x * half, half, LANES)] = wide(
                    ref[:, h * half : (h + 1) * half]
                )

    def down_out(index, ins, outs):
        for ref, x in zip(ins, both(index, 0)):
            outs[0][rows_at(x * half, half), :] = wide(ref[...])

    def attn_out(index, ins, outs):
        for ref, x in zip(ins[:2], both(index, 0)):
            outs[0][rows_at(x * width, width), :] = wide(ref[...])
        for ref, x in zip(ins[2:], both(index, 0)):
            outs[1][x] = wide(ref[...])

    down_x = order(down_x)
    grad_down = run("down_out", [down, down_x], [(units, dim, F32)], down_out)
    vo_z = order(vo_z)
    vo = order(more(*sums(index, [vo, vo_z])))
    vo_x = over(vo, 0)
    up_z = order(up_z)
    grad_up = run("up_out", [up_t, up_z], [(dim, units, F32)], up_out)
    qk_x, vo_x = order(qk_x, vo_x)
    grad_qk, grad_vo = run(
        "attn_out",
        [qk, qk_x, vo, vo_x],
        [(2 * width, dim, F32), (2, width, dim, F32)],
        attn_out,
    )
    grad_qkv = jnp.concatenate([grad_qk, grad_vo[0]])
    grad_qkv = grad_qkv.reshape(3, width, dim).transpose(2, 0, 1)
    return (
        mixed,
        input_grad,
        grad_qkv,
        little[6, :width],
        little[6, width : 2 * width],
        grad_vo[1],
        little[2],
        little[0],
        little[1],
        grad_up,
        little[7],
        grad_down,
        little[5],
        little[3],
        little[4],
    )


def solution(mesh):
    return jax.shard_map(
        local,
        mesh=mesh,
        in_specs=(
            P(("dp", "tensor"), None),
            P(None, None, "tensor"),
            P("tensor"),
            P("tensor"),
            P("tensor", None),
            P(),
            P(),
            P(),
            P(None, "tensor"),
            P("tensor"),
            P("tensor", None),
            P(),
            P(),
            P(),
            P(("dp", "tensor"), None),
            P(("dp", "tensor")),
            P(("dp", "tensor")),
            P("dp", None),
        ),
        out_specs=(
            P(("dp", "tensor"), None),
            P(("dp", "tensor"), None),
            P(None, None, "tensor"),
            P("tensor"),
            P("tensor"),
            P("tensor", None),
            P(),
            P(),
            P(),
            P(None, "tensor"),
            P("tensor"),
            P("tensor", None),
            P(),
            P(),
            P(),
        ),
        check_vma=False,
    )
```

```python
import functools
import math

import jax
import jax.numpy as jnp
from jax import lax
from jax.experimental import pallas as pl
from jax.experimental.pallas import tpu as pltpu
from jax.sharding import PartitionSpec as P

HEAD_DIM = 64
SPAN = 128
LANES = 128
EPSILON = 1e-12
SQRT_HALF = 0.7071067811865476
INV_ROOT_TWO_PI = 0.3989422804014327
SCALE = 1.0 / math.sqrt(HEAD_DIM)
BF = jnp.bfloat16
F32 = jnp.float32
MIB = 1 << 20

CORE, Y = 1, 2


def nn(a, b):
    return lax.dot_general(a, b, (((1,), (0,)), ((), ())), preferred_element_type=F32)


def nt(a, b):
    return lax.dot_general(a, b, (((1,), (1,)), ((), ())), preferred_element_type=F32)


def tn(a, b):
    return lax.dot_general(a, b, (((0,), (0,)), ((), ())), preferred_element_type=F32)


SCALARS = pl.BlockSpec(memory_space=pltpu.SMEM)
WHOLE = pl.BlockSpec(memory_space=pltpu.VMEM)
LEFT = pl.BlockSpec(memory_space=pl.ANY)
FAR = pl.BlockSpec(memory_space=pltpu.HBM)


def call(body, index, args, out, scratch=(), vmem=24, left=(), far=(), cold=(), still=False, name=None):
    count = len(args)
    ranges = dict(far) if isinstance(far, dict) else {i: None for i in far}
    fetched = list(ranges)
    shape_of = {
        i: args[i].shape if ranges[i] is None else (ranges[i][1], *args[i].shape[1:]) for i in fetched
    }
    args = [
        pltpu.with_memory_space_constraint(t, pltpu.HBM) if i in fetched or still and i in left else t
        for i, t in enumerate(args)
    ]
    cold = list(cold)

    def run(index, *refs):
        refs = list(refs)
        del refs[count + 1 + len(out)], refs[count]
        places = refs[count + len(out) :]
        refs = refs[: count + len(out)]
        ins, places = places[: len(fetched)], places[len(fetched) :]
        outs, places = places[: len(cold)], places[len(cold) :]
        sems, rest = places[0], places[1:]
        io = Transfers()
        for j, (i, place) in enumerate(zip(fetched, ins)):
            source = refs[i] if ranges[i] is None else refs[i].at[pl.ds(*ranges[i])]
            io.coming.append((place, pltpu.make_async_copy(source, place, sems.at[j])))
            refs[i] = place
        for j, (i, place) in enumerate(zip(cold, outs)):
            copy = pltpu.make_async_copy(place, refs[count + i], sems.at[len(fetched) + j])
            io.going.append((place, copy))
            refs[count + i] = place
        for _, copy in io.coming:
            copy.start()
        body(io, index, *refs, *rest)
        assert not io.coming, name
        io.push(*outs)
        for copy in io.gone:
            copy.wait()

    places = [pltpu.HBM if i in cold else None for i in range(len(out))]
    *got, index.token = pl.pallas_call(
        run,
        out_shape=[
            jax.ShapeDtypeStruct(s, t) if place is None else place(s, t)
            for (s, t), place in zip(out, places)
        ]
        + [jax.ShapeDtypeStruct(index.token.shape, index.token.dtype)],
        in_specs=[SCALARS]
        + [
            FAR if i in fetched or still and i in left else LEFT if i in left else WHOLE
            for i in range(count)
        ]
        + [LEFT],
        out_specs=[WHOLE if place is None else FAR for place in places] + [LEFT],
        input_output_aliases={count + 1: len(out)},
        scratch_shapes=[pltpu.VMEM(shape_of[i], args[i].dtype) for i in fetched]
        + [pltpu.VMEM(*out[i]) for i in cold]
        + [pltpu.SemaphoreType.DMA((max(len(fetched) + len(cold), 1),))]
        + list(scratch),
        compiler_params=pltpu.CompilerParams(vmem_limit_bytes=vmem * MIB),
        cost_estimate=pl.CostEstimate(flops=1000, bytes_accessed=0, transcendentals=0),
        name=name,
    )(index.scalars, *args, index.token)
    return got


class Kernels:
    def __init__(self, scalars, token):
        self.scalars, self.token = scalars, token


class Transfers:
    def __init__(self):
        self.coming, self.going, self.gone = [], [], []

    def need(self, *refs):
        for place, copy in list(self.coming):
            if any(place is ref for ref in refs):
                copy.wait()
                self.coming = [t for t in self.coming if t[0] is not place]

    def push(self, *refs):
        for place, copy in list(self.going):
            if any(place is ref for ref in refs):
                copy.start()
                self.gone.append(copy)
                self.going = [t for t in self.going if t[0] is not place]


def rows_at(start, size, unit=16):
    return pl.ds(pl.multiple_of(start, unit), size)


def gather_weights(index, halves, w, sems):
    width = w.shape[0] // 8
    pair = 2 * width
    copies = []
    for block in range(2):
        for order in range(2):
            which = index[0] if order == 0 else 1 - index[0]
            for j in range(2):
                start = (2 * which + j) * pair + block * width
                copies.append(
                    pltpu.make_async_copy(
                        halves[2 * block + order].at[pl.ds(j * width, width)],
                        w.at[rows_at(start, width)],
                        sems.at[len(copies)],
                    )
                )
    for copy in copies:
        copy.start()
    return copies


def probs_of(scores):
    expo = jnp.exp(scores - jnp.max(scores, axis=0, keepdims=True))
    return expo * (1.0 / jnp.sum(expo, axis=0, keepdims=True))


def two_heads(value):
    low = lax.broadcasted_iota(jnp.int32, value.shape, 1) < HEAD_DIM
    zero = jnp.zeros_like(value)
    return jnp.concatenate([jnp.where(low, value, zero), jnp.where(low, zero, value)], axis=0)


def of_two_heads(value):
    half = value.shape[0] // 2
    low = lax.broadcasted_iota(jnp.int32, (half, value.shape[1]), 1) < HEAD_DIM
    return jnp.where(low, value[:half], value[half:])


def norm_rows(summed):
    centre = summed - jnp.mean(summed, axis=-1, keepdims=True)
    factor = lax.rsqrt(jnp.mean(centre * centre, axis=-1, keepdims=True) + EPSILON)
    return centre * factor, factor


def norm_back(incoming, normed, factor, gain):
    scaled = incoming * gain
    return factor * (
        scaled
        - jnp.mean(scaled, axis=-1, keepdims=True)
        - normed * jnp.mean(scaled * normed, axis=-1, keepdims=True)
    )


def attend_body(last, io, index, x, w0a, w0b, w1a, w1b, acc, *rest):
    if last:
        norms, q, k, v, ctx, w, acc_out, up_bias, second, first_low, first_turned, vt, rows_of, sems = rest
    else:
        q, k, v, ctx, w, acc_out, up_bias, vt, rows_of, sems = rest
    rows = x.shape[0]
    pair = q.shape[1]
    copies = [
        pltpu.make_async_copy(message.at[pl.ds(pair, SMALL)], rows_of.at[i], sems.at[8 + i])
        for i, message in enumerate((w0a, w1a))
    ]
    for copy in copies:
        copy.start()
    copies += gather_weights(index, (w0a, w0b, w1a, w1b), w, sems)
    for copy in copies:
        copy.wait()
    biases = []
    for i in range(2):
        parts = rows_of[i].astype(F32)
        biases.append(parts[0:2] + parts[2:4] + parts[4:6])
        up_bias[i : i + 1, :] = biases[i][1:2]
    low = lax.broadcasted_iota(jnp.int32, (1, pair), 1) < pair // 2
    query_bias, value_bias = (
        jnp.where(low, biases[0][0:1, cut], biases[1][0:1, cut])
        for cut in (slice(0, pair), slice(pair, 2 * pair))
    )
    query = (nt(x[...], w[:pair, :]) + query_bias).astype(BF)
    q[...] = (query.astype(F32) * SCALE).astype(BF)
    k[...] = nt(x[...], w[pair : 2 * pair, :]).astype(BF)
    value = (nt(x[...], w[2 * pair : 3 * pair, :]) + value_bias).astype(BF)
    v[...] = value
    vt[...] = value.T

    def span(i, _):
        here = rows_at(i * SPAN, SPAN, SPAN)
        for tile in range(pair // LANES):
            cut = slice(tile * LANES, (tile + 1) * LANES)
            scores = nt(two_heads(k[here, cut]), q[here, cut])
            for h in range(2):
                probs = probs_of(scores[h * SPAN : (h + 1) * SPAN])
                own = slice(tile * LANES + h * HEAD_DIM, tile * LANES + (h + 1) * HEAD_DIM)
                ctx[own, here] = nn(vt[own, here], probs.astype(BF)).astype(BF)
        return 0

    io.push(q, k, v, w)
    lax.fori_loop(0, rows // SPAN, span, 0, unroll=2)
    io.push(ctx)
    total = acc[...] + tn(ctx[...], w[3 * pair :, :])
    acc_out[...] = total
    if last:
        normed, _ = norm_rows(total)
        first = normed * norms[0:1, :] + norms[1:2, :]
        low = first.astype(BF)
        first_low[...] = low
        first_turned[...] = low.T
        second[...] = first + norms[2:3, :]


def attend(index, x, halves, acc, norms=None):
    rows, dim = x.shape
    pair = halves[0].shape[0] - SMALL
    last = norms is not None
    args = [x, *halves, acc] + ([norms] if last else [])
    out = [((rows, pair), BF)] * 3 + [((pair, rows), BF), ((4 * pair, dim), BF), ((rows, dim), F32)]
    out += [((2, dim), F32)]
    if last:
        out += [((rows, dim), F32), ((rows, dim), BF), ((dim, rows), BF)]
    return call(
        functools.partial(attend_body, last),
        index,
        args,
        out,
        [
            pltpu.VMEM((pair, rows), BF),
            pltpu.VMEM((2, SMALL, dim), BF),
            pltpu.SemaphoreType.DMA((10,)),
        ],
        left=(1, 2, 3, 4),
        cold=range(5),
        name="attend",
    )


SMALL = 16


def put_small(message, at, value):
    high = value.astype(BF)
    message[at : at + SMALL, :] = high
    message[at + SMALL : at + 2 * SMALL, :] = (value - high.astype(F32)).astype(BF)


def get_small(message, at):
    return message[at : at + SMALL, :].astype(F32) + message[at + SMALL : at + 2 * SMALL, :].astype(F32)


def attend_scores_body(io, index, grad, w_out, k, q, v, dqt, dk, dv, kt, dc):
    rows, pair = k.shape
    io.need(w_out)
    dc[...] = nt(grad[...], w_out[...]).astype(BF)
    io.need(k, q, v)
    kt[...] = k[...].T

    def span(i, _):
        here = rows_at(i * SPAN, SPAN, SPAN)
        for tile in range(pair // LANES):
            cut = slice(tile * LANES, (tile + 1) * LANES)
            query, grads = q[here, cut], dc[here, cut]
            scores = nt(two_heads(k[here, cut]), query)
            d_probs = nt(two_heads(v[here, cut]), grads)
            low_probs, low_scores = [], []
            for h in range(2):
                own_rows = slice(h * SPAN, (h + 1) * SPAN)
                probs = probs_of(scores[own_rows])
                inner = jnp.sum(d_probs[own_rows] * probs, axis=0, keepdims=True)
                d_scores = (probs * (d_probs[own_rows] - inner)).astype(BF)
                low_probs.append(probs.astype(BF))
                low_scores.append(d_scores)
                mine = slice(tile * LANES + h * HEAD_DIM, tile * LANES + (h + 1) * HEAD_DIM)
                dqt[mine, here] = (nn(kt[mine, here], d_scores) * SCALE).astype(BF)
            dk[here, cut] = of_two_heads(nn(jnp.concatenate(low_scores, axis=0), query)).astype(BF)
            dv[here, cut] = of_two_heads(nn(jnp.concatenate(low_probs, axis=0), grads)).astype(BF)
        return 0

    lax.fori_loop(0, rows // SPAN, span, 0, unroll=2)


def attend_scores(index, kept, grad):
    q, k, v, ctx, w = kept
    rows, pair = q.shape
    return call(
        attend_scores_body,
        index,
        [grad, w, k, q, v],
        [((pair, rows), BF), ((rows, pair), BF), ((rows, pair), BF)],
        [pltpu.VMEM((pair, rows), BF), pltpu.VMEM((rows, pair), BF)],
        far={1: (3 * pair, pair), 2: None, 3: None, 4: None},
        name="attend_scores",
    )


def attend_weights_body(last, io, index, ctx, grad, dqt, dk, dv, x, w, acc, *rest):
    if last:
        small0, small1, *rest = rest
    own, *messages, sums, acc_out = rest
    rows = x.shape[0]
    pair = ctx.shape[0]
    width = pair // 2

    def put(part, value):
        value = value.astype(BF)
        own[part] = value[:width]
        per = 4 // len(messages)
        start = part % per * width
        messages[part // per][start : start + width, :] = value[width:]

    put(0, nn(dqt[...], x[...]))
    put(1, tn(dk[...], x[...]))
    put(2, tn(dv[...], x[...]))
    io.need(ctx)
    put(3, nn(ctx[...], grad[...]))
    ones = jnp.ones((8, rows), BF)
    sum_q, sum_v = nt(ones, dqt[...])[0:1], nn(ones, dv[...])[0:1]
    for block in range(2):
        cut = slice(block * width, (block + 1) * width)
        sums[block : block + 1, 0:width] = sum_q[:, cut]
        sums[block : block + 1, width : 2 * width] = sum_v[:, cut]
    if last:
        for block, small in enumerate((small0, small1)):
            small[6:7, 0:pair] = sums[block : block + 1, :]
        put_small(messages[0], 2 * width, small1[...])
    io.need(w)
    acc_out[...] = (
        acc[...]
        + tn(dqt[...], w[:pair, :])
        + nn(dk[...], w[pair : 2 * pair, :])
        + nn(dv[...], w[2 * pair : 3 * pair, :])
    )


def attend_weights(index, kept, grad, parts, x, acc, small=()):
    rows, dim = x.shape
    pair = kept[3].shape[0]
    width = pair // 2
    last = bool(small)

    def body(io, index, *refs):
        if not last:
            return attend_weights_body(False, io, index, *refs)
        ins, (sums_attn, sums_ffn, sums_far), ups, rest = refs[:8], refs[8:11], refs[11:15], refs[15:]
        outs, out0, spare = rest[:5], rest[5], rest[6]
        for block, out in enumerate((out0, spare)):
            out[...] = jnp.zeros_like(out)
            out[0:3, :] = sums_attn[...]
            out[3:6, :] = sums_ffn[...]
            out[7:8, :] = ups[block][0:1, :]
            out[8:9, 0:pair] = sums_far[block : block + 1, :]
            out[9:10, :] = ups[2 + block][0:1, :]
        return attend_weights_body(True, io, index, *ins, out0, spare, *outs)

    out = [((4, width, dim), BF)]
    out += [((pair + 2 * SMALL, dim), BF), ((pair, dim), BF)] if last else [((2 * pair, dim), BF)]
    out += [((2, pair), F32), ((rows, dim), F32)]
    out += [((SMALL, dim), F32)] if last else []
    return call(
        body,
        index,
        [kept[3], grad, *parts, x, kept[4], acc, *small],
        out,
        [pltpu.VMEM((SMALL, dim), F32)] if last else [],
        far={0: None, 6: (0, 3 * pair)},
        name="attend_weights",
    )


def attend_back_body(last, io, index, ctx, grad, w, x, q, k, v, acc, *rest):
    if last:
        small0, small1, *rest = rest
    own, *messages, sums, acc_out, kt, dc, dqt, dk, dv = rest
    rows = x.shape[0]
    pair = ctx.shape[0]
    width = pair // 2

    def put(part, value):
        value = value.astype(BF)
        own[part] = value[:width]
        per = 4 // len(messages)
        start = part % per * width
        messages[part // per][start : start + width, :] = value[width:]

    io.need(ctx, grad)
    put(3, nn(ctx[...], grad[...]))
    io.need(w, x)
    dc[...] = nt(grad[...], w[3 * pair :, :]).astype(BF)
    io.need(q, k, v)
    kt[...] = k[...].T

    def span(i, _):
        here = rows_at(i * SPAN, SPAN, SPAN)
        for tile in range(pair // LANES):
            cut = slice(tile * LANES, (tile + 1) * LANES)
            query, grads = q[here, cut], dc[here, cut]
            scores = nt(two_heads(k[here, cut]), query)
            d_probs = nt(two_heads(v[here, cut]), grads)
            low_probs, low_scores = [], []
            for h in range(2):
                own_rows = slice(h * SPAN, (h + 1) * SPAN)
                probs = probs_of(scores[own_rows])
                inner = jnp.sum(d_probs[own_rows] * probs, axis=0, keepdims=True)
                d_scores = (probs * (d_probs[own_rows] - inner)).astype(BF)
                low_probs.append(probs.astype(BF))
                low_scores.append(d_scores)
                mine = slice(tile * LANES + h * HEAD_DIM, tile * LANES + (h + 1) * HEAD_DIM)
                dqt[mine, here] = (nn(kt[mine, here], d_scores) * SCALE).astype(BF)
            dk[here, cut] = of_two_heads(nn(jnp.concatenate(low_scores, axis=0), query)).astype(BF)
            dv[here, cut] = of_two_heads(nn(jnp.concatenate(low_probs, axis=0), grads)).astype(BF)
        return 0

    lax.fori_loop(0, rows // SPAN, span, 0, unroll=2)
    put(0, nn(dqt[...], x[...]))
    put(1, tn(dk[...], x[...]))
    put(2, tn(dv[...], x[...]))
    ones = jnp.ones((8, rows), BF)
    sum_q, sum_v = nt(ones, dqt[...])[0:1], nn(ones, dv[...])[0:1]
    for block in range(2):
        cut = slice(block * width, (block + 1) * width)
        sums[block : block + 1, 0:width] = sum_q[:, cut]
        sums[block : block + 1, width : 2 * width] = sum_v[:, cut]
    if last:
        for block, small in enumerate((small0, small1)):
            small[6:7, 0:pair] = sums[block : block + 1, :]
        put_small(messages[0], 2 * width, small1[...])
    acc_out[...] = (
        acc[...]
        + tn(dqt[...], w[:pair, :])
        + nn(dk[...], w[pair : 2 * pair, :])
        + nn(dv[...], w[2 * pair : 3 * pair, :])
    )


def attend_back(index, kept, grad, x, acc, small=()):
    rows, dim = x.shape
    pair = kept[3].shape[0]
    width = pair // 2
    last = bool(small)

    def body(io, index, *refs):
        if not last:
            return attend_back_body(False, io, index, *refs)
        ins, (sums_attn, sums_ffn, sums_far), ups, rest = refs[:8], refs[8:11], refs[11:15], refs[15:]
        outs, out0, spare, scratch = rest[:5], rest[5], rest[6], rest[7:]
        for block, out in enumerate((out0, spare)):
            out[...] = jnp.zeros_like(out)
            out[0:3, :] = sums_attn[...]
            out[3:6, :] = sums_ffn[...]
            out[7:8, :] = ups[block][0:1, :]
            out[8:9, 0:pair] = sums_far[block : block + 1, :]
            out[9:10, :] = ups[2 + block][0:1, :]
        return attend_back_body(True, io, index, *ins, out0, spare, *outs, *scratch)

    out = [((4, width, dim), BF)]
    out += [((pair + 2 * SMALL, dim), BF), ((pair, dim), BF)] if last else [((2 * pair, dim), BF)]
    out += [((2, pair), F32), ((rows, dim), F32)]
    out += [((SMALL, dim), F32)] if last else []
    return call(
        body,
        index,
        [kept[3], grad, kept[4], x, *kept[:3], acc, *small],
        out,
        ([pltpu.VMEM((SMALL, dim), F32)] if last else [])
        + [pltpu.VMEM((pair, rows), BF), pltpu.VMEM((rows, pair), BF)]
        + [pltpu.VMEM((pair, rows), BF)]
        + [pltpu.VMEM((rows, pair), BF), pltpu.VMEM((rows, pair), BF)],
        far=(0, 2, 4, 5, 6),
        name="attend_back",
    )


def gelu_parts(upper):
    phi = 0.5 * (1.0 + lax.erf(upper * SQRT_HALF))
    slope = phi + upper * jnp.exp(-0.5 * upper * upper) * INV_ROOT_TWO_PI
    return (upper * phi).astype(BF), slope.astype(BF)


def feed_body(count, io, index, first, *refs):
    weights, acc, bias, refs = refs[: 2 * count], refs[2 * count], refs[2 * count + 1], refs[2 * count + 2 :]
    active, slope, acc_out = refs[:count], refs[count : 2 * count], refs[2 * count]
    total = None
    for i in range(count):
        up, down = weights[2 * i : 2 * i + 2]
        size = up.shape[1]
        step = min(size, 384)
        for at in range(0, size, step):
            cut = slice(at, at + step)
            act, slp = gelu_parts(nn(first[...], up[:, cut]) + bias[i : i + 1, cut])
            active[i][cut, :] = act.T
            slope[i][:, cut] = slp
            more = nn(act, down[cut, :])
            total = more if total is None else total + more
        io.push(active[i], slope[i])
    acc_out[...] = total + acc[...]


def feed(index, first, acc, bias, up, down):
    rows, dim = first.shape
    count, size = len(up), up[0].shape[1]
    out = call(
        functools.partial(feed_body, count),
        index,
        [first, *(t for both in zip(up, down) for t in both), acc, bias],
        [((size, rows), BF)] * count + [((rows, size), BF)] * count + [((rows, dim), F32)],
        name="feed",
    )
    return out[:count], out[count : 2 * count], out[2 * count]


def x_half(index, h, size):
    return rows_at((index[0] if h == 0 else 1 - index[0]) * size, size, LANES)


def feed_up_body(block, io, index, first, *refs):
    up, bias, plain, active, slope = refs[:2], refs[2], refs[3:5], refs[5:7], refs[7:9]
    for h in range(2):
        there = x_half(index, h, up[h].shape[1])
        act, slp = gelu_parts(nn(first[...], up[h][: first.shape[1], :]) + bias[block : block + 1, there])
        plain[h][...] = act
        active[h][...] = act.T
        slope[h][...] = slp


def feed_up(index, first, bias, block, up):
    rows, dim = first.shape
    size = up[0].shape[1]
    out = call(
        functools.partial(feed_up_body, block),
        index,
        [first, *up, bias],
        [((rows, size), BF)] * 2 + [((size, rows), BF)] * 2 + [((rows, size), BF)] * 2,
        name="feed_up",
    )
    return out[:2], out[2:4], out[4:]


def down_dot(index, active, down):
    size = active[0].shape[1]
    first, second = (nn(active[h][...], down[x_half(index, h, size), :]) for h in range(2))
    return first + second


def feed_down(index, acc, active, down):
    def body(io, index, acc, first, second, down, out):
        out[...] = acc[...] + down_dot(index, (first, second), down)

    return call(body, index, [acc, *active, down], [(acc.shape, F32)], name="feed_down")[0]


def down_back_body(near, more, last, io, index, grad, *refs):
    count = 1 if near else 2
    active, refs = refs[:count], refs[count:]
    other, refs = (refs[0], refs[1:]) if more else (None, refs)
    far, refs = (refs[0], refs[1:]) if last else (None, refs)
    out, refs = refs[0], refs[1:]
    half = (out if last else out.at[0]).shape[0]
    if last:
        send, sems = refs
        copy = pltpu.make_async_copy(far.at[1], send.at[0], sems.at[0])
        copy.start()
    for h in range(2):
        if near:
            start = (index[0] if h == 0 else 1 - index[0]) * half
            value = nn(active[0][rows_at(start, half, LANES), :], grad[...])
        else:
            value = nn(active[h][...], grad[...])
        if more:
            value = value + other[h].astype(F32)
        if last and h == 0:
            out[...] = value.astype(BF)
        elif last:
            send[1] = value.astype(BF)
        else:
            out[h] = value.astype(BF)
    if last:
        copy.wait()


def down_back(index, grad, active, other=None, far=None):
    rows, dim = grad.shape
    near = len(active) == 1
    units = sum(t.shape[0] for t in active)
    more, last = other is not None, far is not None
    parts = (2, units // 2, dim)
    args = [grad, *active] + ([other] if more else []) + ([far] if last else [])
    return call(
        functools.partial(down_back_body, near, more, last),
        index,
        args,
        [((units // 2, dim), BF), (parts, BF)] if last else [(parts, BF)],
        [pltpu.SemaphoreType.DMA((1,))] if last else [],
        left=[len(args) - 1] if last else [],
        name="down_back",
    )


def up_back_body(near, more, apart, io, index, grad, *refs):
    count = 1 if near else 2
    down, slope, refs = refs[0], refs[1 : 1 + count], refs[1 + count :]
    first_turned, up, refs = refs[0], refs[1 : 1 + count], refs[1 + count :]
    other, refs = (refs[:2], refs[2:]) if more else ((), refs)
    acc, refs = refs[0], refs[1:]
    g_up, refs = (refs[:2], refs[2:]) if apart else ((refs[0].at[0], refs[0].at[1]), refs[1:])
    sums, acc_out = refs
    half = sums.shape[1] // 2
    size = first_turned.shape[0] // 2
    ones = jnp.ones((8, grad.shape[0]), BF)
    total = acc[...]
    if near:
        d_upper = (nt(grad[...], down[...]) * wide(slope[0][...])).astype(BF)
        sums[...] = nn(ones, d_upper)
        for z in range(2):
            rows = rows_at((index[1] if z == 0 else 1 - index[1]) * size, size, LANES)
            value = nn(first_turned[rows, :], d_upper)
            for h in range(2):
                cut = slice(h * half, (h + 1) * half)

                @pl.when(index[0] == 0)
                def _():
                    own = value[:, cut]
                    if more:
                        own = own + other[z][:, cut].astype(F32)
                    g_up[z][:, cut] = own.astype(BF)

                @pl.when(index[0] == 1)
                def _():
                    own = value[:, (1 - h) * half : (2 - h) * half]
                    if more:
                        own = own + other[z][:, cut].astype(F32)
                    g_up[z][:, cut] = own.astype(BF)

        acc_out[...] = total + nt(d_upper, up[0][...])
        return
    for h in range(2):
        there = x_half(index, h, half)
        cut = slice(h * half, (h + 1) * half)
        slp = wide(slope[h][...])
        d_upper = (nt(grad[...], down[there, :]) * slp).astype(BF)
        sums[:, there] = nn(ones, d_upper)
        for z in range(2):
            rows = rows_at((index[1] if z == 0 else 1 - index[1]) * size, size, LANES)
            value = nn(first_turned[rows, :], d_upper)
            if more:
                value = value + other[z][:, cut].astype(F32)
            g_up[z][:, cut] = value.astype(BF)
        total = total + nt(d_upper, up[h][: acc.shape[1], :])
    acc_out[...] = total


def up_back(index, first_turned, grad, acc, slope, up, down, other=(), apart=False):
    rows, dim = grad.shape
    near = len(up) == 1
    units = down.shape[0]
    half = (dim // 2, units)
    *got, sums, total = call(
        functools.partial(up_back_body, near, bool(other), apart),
        index,
        [grad, down, *slope, first_turned, *up, *other, acc],
        ([(half, BF)] * 2 if apart else [((2, *half), BF)])
        + [((8, units), F32), ((rows, dim), F32)],
        name="up_back",
    )
    return got, sums, total


def pack_body(io, index, qkv, output, w_up, biases, first, second, up_half, sems):
    width = output.shape[0]
    there = rows_at(index[0] * up_half.shape[1], up_half.shape[1], LANES)
    up_copy = pltpu.make_async_copy(
        w_up.at[:, there], up_half.at[pl.ds(0, w_up.shape[0])], sems.at[4]
    )

    def copies(x):
        for part in range(4):
            source = output if part == 3 else qkv.at[pl.ds(part * width, width)]
            place = first if part // 2 == x else second
            place = place.at[pl.ds(part % 2 * width, width)]
            yield pltpu.make_async_copy(source, place, sems.at[part])

    for x in range(2):

        @pl.when(index[0] == x)
        def _():
            for copy in copies(x):
                copy.start()
            up_copy.start()
            rest = biases[...]
            parts = []
            for _ in range(3):
                parts.append(rest.astype(BF).astype(F32))
                rest = rest - parts[-1]
            parts.append(jnp.zeros((SMALL - 6, rest.shape[1]), F32))
            first[2 * width :, :] = jnp.concatenate(parts, axis=0).astype(BF)
            for copy in copies(x):
                copy.wait()
            up_copy.wait()


def pack(index, qkv, output, w_up, biases):
    width, dim = output.shape
    out = [((2 * width + SMALL, dim), BF), ((2 * width, dim), BF), ((dim + 32, w_up.shape[1] // 2), BF)]
    return call(
        pack_body,
        index,
        [qkv, output, w_up, biases],
        out,
        [pltpu.SemaphoreType.DMA((5,))],
        left=(0, 1, 2),
        still=True,
        name="pack",
    )


def turn_body(io, index, first, second, down, acc, out_grad, cls_rows, norms, *refs):
    mixed, d_second, low, sums = refs
    second = acc[...] + down_dot(index, (first, second), down)
    normed, factor = norm_rows(second)
    mixed[...] = (normed * norms[0:1, :] + norms[1:2, :]).astype(BF)
    spans = cls_rows.shape[0]
    shape = (spans, SPAN, out_grad.shape[1])
    first_row = lax.broadcasted_iota(jnp.int32, shape, 1) == 0
    incoming = wide(out_grad[...]).reshape(shape)
    incoming = incoming + jnp.where(first_row, cls_rows[...][:, None, :], 0.0)
    incoming = incoming.reshape(out_grad.shape)
    grad = norm_back(incoming, normed, factor, norms[0:1, :])
    d_second[...] = grad
    low[...] = grad.astype(BF)
    sums[0:1, :] = jnp.sum(incoming * normed, axis=0, keepdims=True)
    sums[1:2, :] = jnp.sum(incoming, axis=0, keepdims=True)
    sums[2:3, :] = jnp.sum(grad.astype(BF).astype(F32), axis=0, keepdims=True)


def turn(index, acc, cotangent, norms, active, down):
    size = acc.shape
    return call(
        turn_body,
        index,
        [*active, down, acc, *cotangent, norms],
        [(size, BF), (size, F32), (size, BF), ((3, size[1]), F32)],
        name="turn",
    )


def first_back_body(io, index, attended, incoming, norms, d_attn, low, sums):
    normed, factor = norm_rows(attended[...])
    grad = norm_back(incoming[...], normed, factor, norms[0:1, :])
    d_attn[...] = grad
    low[...] = grad.astype(BF)
    sums[0:1, :] = jnp.sum(incoming[...] * normed, axis=0, keepdims=True)
    sums[1:2, :] = jnp.sum(incoming[...], axis=0, keepdims=True)
    sums[2:3, :] = jnp.sum(grad.astype(BF).astype(F32), axis=0, keepdims=True)


def first_back(index, attended, incoming, norms):
    size = attended.shape
    return call(
        first_back_body,
        index,
        [attended, incoming, norms],
        [(size, F32), (size, BF), ((3, size[1]), F32)],
        name="first_back",
    )


def wide(value):
    return value.astype(F32)


def blocks(index, args, out, body, name="blocks"):
    def run(io, index, *refs):
        body(index, refs[: len(args)], refs[len(args) :])

    return call(run, index, args, out, name=name)


def sums(index, *groups):
    def body(_, ins, outs):
        at = 0
        for group, out in zip(groups, outs):
            total = wide(ins[at][...])
            for i in range(1, len(group)):
                total = total + wide(ins[at + i][...])
            out[...] = total.astype(BF)
            at += len(group)

    return blocks(
        index,
        [a for group in groups for a in group],
        [(group[0].shape, BF) for group in groups],
        body,
        name="sums",
    )


def split_sum(index, which, a, b):
    half = a.shape[0] // 2

    def body(index, ins, outs):
        for out, bit in zip(outs, (index[which], 1 - index[which])):
            there = rows_at(bit * half, half)
            out[...] = (wide(ins[0][there, :]) + wide(ins[1][there, :])).astype(BF)

    return blocks(index, [a, b], [((half, a.shape[1]), BF)] * 2, body, name="split_sum")


def join(index, which, own, other):
    half = own.shape[0]

    def body(index, ins, outs):
        for value, bit in zip(ins, (index[which], 1 - index[which])):
            outs[0][rows_at(bit * half, half), :] = value[...]

    return blocks(index, [own, other], [((2 * half, own.shape[1]), BF)], body, name="join")[0]


def swap(value, axis, bit):
    size = lax.axis_size(axis)
    return lax.ppermute(value, axis, [(i, i ^ bit) for i in range(size)])


class Order:
    def __init__(self, token):
        self.token = token

    def __call__(self, *values):
        self.token, *values = lax.optimization_barrier((self.token, *values))
        return values[0] if len(values) == 1 else values


STEPS = (None, "D", None, "UDQVDVUQDVUVQDQUVQQUDVVUQ")
PATHS = {"D": "xz", "U": "yz", "Q": "xz", "V": "Z"}


def pick_half(value, index, axis=0):
    half = value.shape[axis] // 2
    return lax.dynamic_slice_in_dim(value, index * half, half, axis)


def local(
    inputs,
    w_qkv,
    bias_query,
    bias_value,
    w_output,
    bias_output,
    gain_attn,
    shift_attn,
    w_up,
    bias_up,
    w_down,
    bias_down,
    gain_ffn,
    shift_ffn,
    out_grad,
    mlm_mask,
    span_doc,
    cls_grad,
):
    rows, dim = inputs.shape
    width = w_qkv.shape[2]
    units = w_up.shape[1]
    half = units // 2
    dp = lax.axis_index("dp")
    bits = [1 << i for i in range(lax.axis_size("dp").bit_length() - 1)]
    ix = dp % 2
    scalars = jnp.stack([ix, (dp // bits[1]) % 2, (dp // bits[2]) % 2]).astype(jnp.int32)
    index = Kernels(scalars, jnp.zeros((8, LANES), F32))
    order = Order(bias_output)

    def core(value):
        return swap(value, "tensor", CORE)

    def over_y(value):
        return swap(value, "tensor", Y)

    def over(value, n):
        return swap(value, "dp", bits[n])

    biases = jnp.concatenate([bias_query, bias_query, bias_value, bias_value, bias_up])
    *own, up_send = pack(
        index,
        w_qkv.transpose(1, 2, 0).reshape(3 * width, dim),
        w_output,
        w_up,
        biases.reshape(2, dim),
    )
    attn = {0: tuple(own)}
    attn_a = over_y(own[0])
    attn[1] = tuple(core(t) for t in own)
    up_a = over_y(up_send)

    norms_attn = jnp.stack([gain_attn, shift_attn, bias_down])
    norms_ffn = jnp.stack([gain_ffn, shift_ffn])
    kept = {}
    attended = bias_output + inputs.astype(F32)

    weighting = jnp.where(mlm_mask == 1, 2.0, 0.5).astype(BF)
    docs_here = cls_grad.shape[0]
    local_doc = span_doc - dp * docs_here
    picker = (local_doc[:, None] == jnp.arange(docs_here, dtype=jnp.int32)[None, :]).astype(F32)
    cls_rows = jnp.dot(picker, cls_grad.astype(F32), precision=lax.Precision.HIGHEST)
    cotangent = [out_grad * weighting[:, None], cls_rows]

    up, down = {0: w_up, 1: core(w_up)}, {0: w_down, 1: core(w_down)}
    near = order(*attn[0], *attn[1], attended)
    attn[0], attn[1], attended = tuple(near[:2]), tuple(near[2:4]), near[4]
    *kept[0], attended, up_bias = attend(index, inputs, attn[0] + attn[1], attended)

    attended, attn_a, up[1], down[1], w_down, *cotangent = order(
        attended, attn_a, up[1], down[1], w_down, *cotangent
    )
    attn_b = over(attn_a, 0)
    far_a = core(attn_a)
    down[2] = over_y(w_down)
    up_a = order(up_a)
    up_b = over(up_a, 0)
    up_far_a = core(up_a)
    attn_b, far_a = order(attn_b, far_a)
    far_b, up_far_a = order(core(attn_b), up_far_a)
    attn[2], attn[3] = (attn_a, attn_b), (far_a, far_b)
    *kept[2], attended, up_bias_far, second, first_low, first_turned = attend(
        index, inputs, attn[2] + attn[3], attended, norms_attn
    )

    act_near, slope_near, second = feed(
        index, first_low, second, up_bias, [up[0], up[1]], [down[0], down[1]]
    )
    second, up_b = order(second, up_b)
    up_far_b = core(up_b)
    plain_2, act_2, slope_2 = feed_up(index, first_low, up_bias_far, 0, [up_a, up_b])
    *plain_2, down[2] = order(*plain_2, down[2])
    down[3] = core(down[2])
    second, up_far_b = order(feed_down(index, second, plain_2, down[2]), up_far_b)
    plain_3, act_3, slope_3 = feed_up(index, first_low, up_bias_far, 1, [up_far_a, up_far_b])
    *plain_3, down[3] = order(*plain_3, down[3])
    mixed, d_second, branch_grad, sums_ffn = turn(
        index, second, cotangent, norms_ffn, plain_3, down[3]
    )

    g_bias_up = {}
    act_of = [[act_near[0]], [act_near[1]], act_2, act_3]
    slope_of = [[slope_near[0]], [slope_near[1]], slope_2, slope_3]
    up_of = [[up[0]], [up[1]], [up_a, up_b], [up_far_a, up_far_b]]

    def back_up(r, total, other=(), apart=False):
        got, g_bias_up[r], total = up_back(
            index, first_turned, branch_grad, total, slope_of[r], up_of[r], down[r], other, apart
        )
        return order(*got, total)

    def add(*values):
        total = wide(values[0])
        for value in values[1:]:
            total = total + wide(value)
        return total.astype(BF)

    def more(value):
        for n in range(3, len(bits)):
            value = sums(index, [value, over(value, n)])[0]
        return value

    def run(name, args, out, body):
        dtypes = [(t[:-1], F32) if t[-1] == F32 else (t, BF) for t in out]
        return order(*blocks(index, args, dtypes, body, name=name))

    def both(index, n):
        return index[n], 1 - index[n]

    part = width // 2
    extra = 2 * SMALL
    rows_small = (SMALL, dim, F32)
    result = {}

    def down_sum():
        size = half // 2
        quarter = (size, dim)

        def down_1(index, ins, outs):
            far, near, came = ins
            for i, bit in enumerate(both(index, 1)):
                there = rows_at(bit * size, size)
                for j, mine in enumerate((far.at[0], near)):
                    place = outs[j] if i == 0 else outs[2].at[j]
                    place[...] = add(mine[there, :], came[j, there, :])

        def down_2(_, ins, outs):
            for i in range(2):
                outs[i][...] = add(ins[i][...], ins[2][i])

        def down_out(index, ins, outs):
            for ref, x in zip(ins, both(index, 0)):
                outs[0][rows_at(x * half, half), :] = wide(ref[...])

        def down_1y(_, ins, outs):
            far, near, came = ins
            outs[0][...] = add(far[0], came[0])
            outs[1][...] = add(near[...], came[1])

        came = yield over(down_send, 0)
        if PATHS["D"] == "xz":
            f, n, s = run(
                "down_1", [far_down, near_down, came], [quarter, quarter, (2, *quarter)], down_1
            )
            came = yield over(s, 1)
            f, n = run("down_2", [f, n, came], [quarter] * 2, down_2)
            came = yield over_y(f)
            t = order(*sums(index, [n, came]))
        else:
            f, n = run("down_1", [far_down, near_down, came], [(half, dim)] * 2, down_1y)
            came = yield over_y(f)
            k, s = order(*split_sum(index, 1, n, came))
            came = yield over(s, 1)
            t = order(*sums(index, [k, came]))
        came = yield over(t, 2)
        t = order(more(*sums(index, [t, came])))
        came = yield over(t, 1)
        t = order(join(index, 1, t, came))
        came = yield over(t, 0)
        result["down"] = run("down_out", [t, came], [(units, dim, F32)], down_out)

    def up_sum():
        def up_1(_, ins, outs):
            for i in range(2):
                outs[i][...] = add(ins[0][i], ins[1][i])

        def up_2(_, ins, outs):
            for out, cut in zip(outs, (slice(0, half), slice(half, None))):
                out[...] = add(ins[0][:, cut], ins[1][:, cut])

        def up_5(_, ins, outs):
            for i in range(2):
                outs[0][:, i * half : (i + 1) * half] = ins[i][...]

        def up_out(index, ins, outs):
            for ref, z in zip(ins, both(index, 1)):
                rows_here = rows_at(z * (dim // 2), dim // 2)
                for h, x in enumerate(both(index, 0)):
                    outs[0][rows_here, rows_at(x * half, half, LANES)] = wide(
                        ref[:, h * half : (h + 1) * half]
                    )

        def up_1x(_, ins, outs):
            for i in range(2):
                for out, cut in zip(outs, (slice(0, half), slice(half, None))):
                    out[i] = add(ins[0][i, :, cut], ins[1][i, :, cut])

        def up_5x(_, ins, outs):
            for i in range(2):
                outs[0][i] = ins[i][...]

        def up_out_x(index, ins, outs):
            for ref, x in zip(ins, both(index, 0)):
                for i, z in enumerate(both(index, 1)):
                    outs[0][rows_at(z * (dim // 2), dim // 2), rows_at(x * half, half, LANES)] = wide(
                        ref[i]
                    )

        came = yield over_y(far_up)
        if PATHS["U"] == "yx":
            pair_of = (2, dim // 2, half)
            k, s = run("up_1", [near_up, came], [pair_of] * 2, up_1x)
            came = yield over(s, 0)
            k, s = run("up_2", [k, came], [pair_of[1:]] * 2, up_1)
            came = yield over(s, 1)
            t = order(*sums(index, [k, came]))
            came = yield over(t, 2)
            t = order(more(*sums(index, [t, came])))
            came = yield over(t, 1)
            t = run("up_5", [t, came], [pair_of], up_5x)
            came = yield over(t, 0)
            result["up"] = run("up_out", [t, came], [(dim, units, F32)], up_out_x)
            return
        k, s = run("up_1", [near_up, came], [(dim // 2, units)] * 2, up_1)
        came = yield over(s, 1)
        k, s = run("up_2", [k, came], [(dim // 2, half)] * 2, up_2)
        came = yield over(s, 0)
        t = order(*sums(index, [k, came]))
        came = yield over(t, 2)
        t = order(more(*sums(index, [t, came])))
        came = yield over(t, 0)
        t = run("up_5", [t, came], [(dim // 2, units)], up_5)
        came = yield over(t, 1)
        result["up"] = run("up_out", [t, came], [(dim, units, F32)], up_out)

    def rows_of(part):
        return slice(part * width, (part + 1) * width)

    def qk_sum(far, near, far_came, near_came, little):
        def qk_1(index, ins, outs):
            far, near, far_came, near_came, little = ins
            for i, bit in enumerate(both(index, 0)):
                for j, (mine, came) in enumerate(((far, far_came), (near, near_came))):
                    for k in range(2):

                        @pl.when(bit == k)
                        def _():
                            value = add(mine[k], came[rows_of(k), :])
                            if i == 0:
                                outs[j][...] = value
                            else:
                                outs[2][rows_of(j), :] = value

            total = little[...] + get_small(near_came, 2 * width)
            outs[3][...] = total
            put_small(outs[2], 2 * width, total)

        def qk_2(index, ins, outs):
            far, near, came, little = ins
            for i, bit in enumerate(both(index, 1)):
                there = rows_at(bit * part, part)
                for j, mine in enumerate((far, near)):
                    value = add(mine[there, :], came[rows_at(j * width + bit * part, part), :])
                    if i == 0:
                        outs[j][...] = value
                    else:
                        outs[2][j * part : (j + 1) * part, :] = value
            total = little[...] + get_small(came, 2 * width)
            outs[3][...] = total
            put_small(outs[2], 2 * part, total)

        def qk_3(_, ins, outs):
            far, near, came, little = ins
            outs[0][:part, :] = add(far[...], came[:part, :])
            outs[1][...] = add(near[...], came[part : 2 * part, :])
            total = little[...] + get_small(came, 2 * part)
            outs[2][...] = total
            outs[3][...] = jnp.zeros_like(total)
            outs[3][0:6, :] = total[0:6]
            outs[3][6:8, :] = total[8:10]
            put_small(outs[0], part, outs[3][...])

        def qk_4(_, ins, outs):
            mine, came, little = ins
            outs[0][:part, :] = add(mine[...], came[:part, :])
            total = little[...] + get_small(came, part)
            outs[1][...] = total
            put_small(outs[0], part, total)

        def qk_5(_, ins, outs):
            mine, came, little = ins
            outs[0][...] = add(mine[:part, :], came[:part, :])
            outs[1][...] = little[...] + get_small(came, part)

        near_came = yield near_came
        f, n, s, little = run(
            "qk_1",
            [far, near, far_came, near_came, little],
            [(width, dim), (width, dim), (2 * width + extra, dim), rows_small],
            qk_1,
        )
        def qk_2y(_, ins, outs):
            far, near, came, little = ins
            outs[0][:width, :] = add(far[...], came[rows_of(0), :])
            outs[1][...] = add(near[...], came[rows_of(1), :])
            total = little[...] + get_small(came, 2 * width)
            outs[2][...] = total
            outs[3][...] = jnp.zeros_like(total)
            outs[3][0:6, :] = total[0:6]
            outs[3][6:8, :] = total[8:10]
            put_small(outs[0], width, outs[3][...])

        def qk_3y(index, ins, outs):
            mine, came, little = ins
            for bit, out in zip(both(index, 1), outs):
                there = rows_at(bit * part, part)
                out[:part, :] = add(mine[there, :], came[there, :])
            total = little[...] + get_small(came, width)
            outs[2][...] = total
            put_small(outs[1], part, total)

        came = yield over(s, 0)
        if PATHS["Q"] == "xy":
            f, n, little, _ = run(
                "qk_2",
                [f, n, came, little],
                [(width + extra, dim), (width, dim), rows_small, rows_small],
                qk_2y,
            )
            came = yield over_y(f)
            k, s, little = run(
                "qk_3", [n, came, little], [(part, dim), (part + extra, dim), rows_small], qk_3y
            )
            came = yield over(s, 1)
            t, little = run("qk_4", [k, came, little], [(part + extra, dim), rows_small], qk_4)
            came = yield over(t, 2)
            t, little = run("qk_5", [t, came, little], [(part, dim), rows_small], qk_5)
            t = more(t)
            for n in range(3, len(bits)):
                little = little + over(little, n)
            result["little"] = little
            came = yield over(t, 1)
            t = order(join(index, 1, t, came))
            came = yield over(t, 0)
            result["qk"] = (t, came)
            return
        f, n, s, little = run(
            "qk_2",
            [f, n, came, little],
            [(part, dim), (part, dim), (2 * part + extra, dim), rows_small],
            qk_2,
        )
        came = yield over(s, 1)
        f, n, little, _ = run(
            "qk_3",
            [f, n, came, little],
            [(part + extra, dim), (part, dim), rows_small, rows_small],
            qk_3,
        )
        came = yield over_y(f)
        t, little = run("qk_4", [n, came, little], [(part + extra, dim), rows_small], qk_4)
        came = yield over(t, 2)
        t, little = run("qk_5", [t, came, little], [(part, dim), rows_small], qk_5)
        t = more(t)
        for n in range(3, len(bits)):
            little = little + over(little, n)
        result["little"] = little
        came = yield over(t, 1)
        t = order(join(index, 1, t, came))
        came = yield over(t, 0)
        result["qk"] = (t, came)

    def vo_sum(far, near, far_came, near_came):
        def vo_1(_, ins, outs):
            far, near, far_came, near_came = ins
            for k in range(2):
                outs[0][rows_of(k), :] = add(far[2 + k], far_came[rows_of(2 + k), :])
                outs[1][rows_of(k), :] = add(near[2 + k], near_came[rows_of(k), :])

        near_came = yield near_came
        f, n = run("vo_1", [far, near, far_came, near_came], [(2 * width, dim)] * 2, vo_1)
        f = yield f
        came = yield over_y(f)
        k, s = order(*split_sum(index, 0, n, came))
        came = yield over(s, 0)
        if PATHS["V"] == "R":
            k, s = order(*split_sum(index, 1, k, came))
            came = yield over(s, 1)
            t = order(*sums(index, [k, came]))
            came = yield over(t, 2)
            t = order(more(*sums(index, [t, came])))
            came = yield over(t, 1)
            t = order(join(index, 1, t, came))
            came = yield over(t, 0)
            result["vo"] = (t, came)
            return
        t = order(*sums(index, [k, came]))
        came = yield over(t, 1)
        t = order(*sums(index, [t, came]))
        came = yield over(t, 2)
        t = order(more(*sums(index, [t, came])))
        came = yield over(t, 0)
        result["vo"] = (t, came)

    chains, waiting = {}, {}

    def start(name, chain):
        chains[name] = chain
        waiting[name] = next(chain)

    def go(names, arrived=None):
        for name in names:
            if name not in waiting:
                continue
            value = waiting.pop(name) if arrived else order(waiting.pop(name))
            try:
                waiting[name] = chains[name].send(value)
            except StopIteration:
                pass

    down_3 = core(order(*down_back(index, branch_grad, act_of[3])))
    down_1 = core(order(*down_back(index, branch_grad, act_of[1])))
    *up_3, d_first = back_up(3, d_second, apart=True)
    up_3 = [core(t) for t in up_3]
    down_3 = order(down_3)
    far_down = order(*down_back(index, branch_grad, act_of[2], down_3))
    down_1 = order(down_1)
    near_down, down_send = order(*down_back(index, branch_grad, act_of[0], down_1, far_down))
    start("D", down_sum())
    *up_1, d_first = back_up(1, order(d_first), apart=True)
    up_3 = order(*up_3)
    up_1 = [core(t) for t in up_1]
    far_up, d_first = back_up(2, d_first, up_3)
    start("U", up_sum())
    up_1 = order(*up_1)
    near_up, d_first = back_up(0, d_first, up_1)

    d_attn, attended_grad, sums_attn = first_back(index, attended, d_first, norms_attn)

    def attention_back(r, total, between, small=()):
        if between is None:
            return order(*attend_back(index, kept[r], attended_grad, inputs, total, small))
        parts = order(*attend_scores(index, kept[r], attended_grad))
        go(between)
        *parts, total = order(*parts, total)
        out = order(*attend_weights(index, kept[r], attended_grad, parts, inputs, total, small))
        return out

    far_attn, *messages, sums_far, input_grad = attention_back(2, d_attn, STEPS[0])
    waiting["D"], input_grad, *messages = order(waiting["D"], input_grad, *messages)
    from_core = [core(t) for t in messages]
    go("D", True)
    input_grad = order(input_grad)
    near_attn, *to_core, _, input_grad, little = attention_back(
        0,
        input_grad,
        STEPS[2],
        (sums_attn, sums_ffn, sums_far, *(g_bias_up[r] for r in range(4))),
    )
    to_core = [core(t) for t in to_core]
    if STEPS[3][0] in waiting:
        from_core, waiting[STEPS[3][0]] = order(*from_core, waiting[STEPS[3][0]])
    else:
        from_core = order(*from_core)
    start("Q", qk_sum(far_attn, near_attn, from_core, to_core[0], little))
    start("V", vo_sum(far_attn, near_attn, from_core, to_core[1]))
    go(STEPS[3])
    while waiting:
        go([*waiting])

    def attn_out(index, ins, outs):
        qk, vo = ins[:2], ins[2:]
        for ref, x in zip(qk, both(index, 0)):
            outs[0][rows_at(x * width, width), :] = wide(ref[...])
        for x in range(2):

            @pl.when(index[0] == x)
            def _():
                outs[0][rows_of(2), :] = wide(vo[x][...])
                outs[1][...] = wide(vo[1 - x][...])

    grad_down, grad_up, little = result["down"], result["up"], result["little"]
    grad_qkv, grad_output = run(
        "attn_out",
        [*result["qk"], *result["vo"]],
        [(3 * width, dim, F32), (width, dim, F32)],
        attn_out,
    )
    grad_qkv = grad_qkv.reshape(3, width, dim).transpose(2, 0, 1)
    return (
        mixed,
        input_grad,
        grad_qkv,
        little[6, :width],
        little[6, width : 2 * width],
        grad_output,
        little[2],
        little[0],
        little[1],
        grad_up,
        little[7],
        grad_down,
        little[5],
        little[3],
        little[4],
    )


def solution(mesh):
    return jax.shard_map(
        local,
        mesh=mesh,
        in_specs=(
            P(("dp", "tensor"), None),
            P(None, None, "tensor"),
            P("tensor"),
            P("tensor"),
            P("tensor", None),
            P(),
            P(),
            P(),
            P(None, "tensor"),
            P("tensor"),
            P("tensor", None),
            P(),
            P(),
            P(),
            P(("dp", "tensor"), None),
            P(("dp", "tensor")),
            P(("dp", "tensor")),
            P("dp", None),
        ),
        out_specs=(
            P(("dp", "tensor"), None),
            P(("dp", "tensor"), None),
            P(None, None, "tensor"),
            P("tensor"),
            P("tensor"),
            P("tensor", None),
            P(),
            P(),
            P(),
            P(None, "tensor"),
            P("tensor"),
            P("tensor", None),
            P(),
            P(),
            P(),
        ),
        check_vma=False,
    )
```

```python
import functools
import math

import jax
import jax.numpy as jnp
from jax import lax
from jax.experimental import pallas as pl
from jax.experimental.pallas import tpu as pltpu
from jax.sharding import PartitionSpec as P

HEAD_DIM = 64
SPAN = 128
LANES = 128
EPSILON = 1e-12
SQRT_HALF = 0.7071067811865476
INV_ROOT_TWO_PI = 0.3989422804014327
SCALE = 1.0 / math.sqrt(HEAD_DIM)
BF = jnp.bfloat16
F32 = jnp.float32
MIB = 1 << 20

CORE, Y = 1, 2


def nn(a, b):
    return lax.dot_general(a, b, (((1,), (0,)), ((), ())), preferred_element_type=F32)


def nt(a, b):
    return lax.dot_general(a, b, (((1,), (1,)), ((), ())), preferred_element_type=F32)


def tn(a, b):
    return lax.dot_general(a, b, (((0,), (0,)), ((), ())), preferred_element_type=F32)


SCALARS = pl.BlockSpec(memory_space=pltpu.SMEM)
WHOLE = pl.BlockSpec(memory_space=pltpu.VMEM)
LEFT = pl.BlockSpec(memory_space=pl.ANY)
FAR = pl.BlockSpec(memory_space=pltpu.HBM)
PIECES = 4


def call(body, index, args, out, scratch=(), vmem=24, left=(), far=(), cold=(), still=False, name=None):
    count = len(args)
    ranges = dict(far) if isinstance(far, dict) else {i: None for i in far}
    fetched = list(ranges)
    shape_of = {
        i: args[i].shape if ranges[i] is None else (ranges[i][1], *args[i].shape[1:]) for i in fetched
    }
    args = [
        pltpu.with_memory_space_constraint(t, pltpu.HBM) if i in fetched or still and i in left else t
        for i, t in enumerate(args)
    ]
    cold = list(cold)

    def run(index, *refs):
        refs = list(refs)
        del refs[count + 1 + len(out)], refs[count]
        places = refs[count + len(out) :]
        refs = refs[: count + len(out)]
        ins, places = places[: len(fetched)], places[len(fetched) :]
        outs, places = places[: len(cold)], places[len(cold) :]
        sems, rest = places[0], places[1:]
        io = Transfers()
        for j, (i, place) in enumerate(zip(fetched, ins)):
            source = refs[i] if ranges[i] is None else refs[i].at[pl.ds(*ranges[i])]
            io.coming.append((place, pltpu.make_async_copy(source, place, sems.at[j])))
            refs[i] = place
        for j, (i, place) in enumerate(zip(cold, outs)):
            size = place.shape[0] // PIECES
            for k in range(PIECES):
                cut = pl.ds(k * size, size)
                sem = sems.at[len(fetched) + PIECES * j + k]
                copy = pltpu.make_async_copy(place.at[cut], refs[count + i].at[cut], sem)
                io.going.append((place, copy))
            refs[count + i] = place
        for _, copy in io.coming:
            copy.start()
        body(io, index, *refs, *rest)
        assert not io.coming, name
        io.push(*outs)
        for copy in io.gone:
            copy.wait()

    places = [pltpu.HBM if i in cold else None for i in range(len(out))]
    *got, index.token = pl.pallas_call(
        run,
        out_shape=[
            jax.ShapeDtypeStruct(s, t) if place is None else place(s, t)
            for (s, t), place in zip(out, places)
        ]
        + [jax.ShapeDtypeStruct(index.token.shape, index.token.dtype)],
        in_specs=[SCALARS]
        + [
            FAR if i in fetched or still and i in left else LEFT if i in left else WHOLE
            for i in range(count)
        ]
        + [LEFT],
        out_specs=[WHOLE if place is None else FAR for place in places] + [LEFT],
        input_output_aliases={count + 1: len(out)},
        scratch_shapes=[pltpu.VMEM(shape_of[i], args[i].dtype) for i in fetched]
        + [pltpu.VMEM(*out[i]) for i in cold]
        + [pltpu.SemaphoreType.DMA((max(len(fetched) + PIECES * len(cold), 1),))]
        + list(scratch),
        compiler_params=pltpu.CompilerParams(vmem_limit_bytes=vmem * MIB),
        cost_estimate=pl.CostEstimate(flops=1000, bytes_accessed=0, transcendentals=0),
        name=name,
    )(index.scalars, *args, index.token)
    return got


class Kernels:
    def __init__(self, scalars, token):
        self.scalars, self.token = scalars, token


class Transfers:
    def __init__(self):
        self.coming, self.going, self.gone = [], [], []

    def need(self, *refs):
        for place, copy in list(self.coming):
            if any(place is ref for ref in refs):
                copy.wait()
                self.coming = [t for t in self.coming if t[0] is not place]

    def push(self, *refs):
        for place, copy in list(self.going):
            if any(place is ref for ref in refs):
                copy.start()
                self.gone.append(copy)
        self.going = [t for t in self.going if not any(t[0] is ref for ref in refs)]


def rows_at(start, size, unit=16):
    return pl.ds(pl.multiple_of(start, unit), size)


def gather_weights(index, halves, w, sems):
    width = w.shape[0] // 8
    pair = 2 * width
    copies = []
    for block in range(2):
        for order in range(2):
            which = index[0] if order == 0 else 1 - index[0]
            for j in range(2):
                start = (2 * which + j) * pair + block * width
                copies.append(
                    pltpu.make_async_copy(
                        halves[2 * block + order].at[pl.ds(j * width, width)],
                        w.at[rows_at(start, width)],
                        sems.at[len(copies)],
                    )
                )
    for copy in copies:
        copy.start()
    return copies


def probs_of(scores):
    expo = jnp.exp(scores - jnp.max(scores, axis=0, keepdims=True))
    return expo * (1.0 / jnp.sum(expo, axis=0, keepdims=True))


def two_heads(value):
    low = lax.broadcasted_iota(jnp.int32, value.shape, 1) < HEAD_DIM
    zero = jnp.zeros_like(value)
    return jnp.concatenate([jnp.where(low, value, zero), jnp.where(low, zero, value)], axis=0)


def of_two_heads(value):
    half = value.shape[0] // 2
    low = lax.broadcasted_iota(jnp.int32, (half, value.shape[1]), 1) < HEAD_DIM
    return jnp.where(low, value[:half], value[half:])


def norm_rows(summed):
    centre = summed - jnp.mean(summed, axis=-1, keepdims=True)
    factor = lax.rsqrt(jnp.mean(centre * centre, axis=-1, keepdims=True) + EPSILON)
    return centre * factor, factor


def norm_back(incoming, normed, factor, gain):
    scaled = incoming * gain
    return factor * (
        scaled
        - jnp.mean(scaled, axis=-1, keepdims=True)
        - normed * jnp.mean(scaled * normed, axis=-1, keepdims=True)
    )


def attend_body(last, io, index, x, w0a, w0b, w1a, w1b, acc, *rest):
    if last:
        norms, q, k, v, ctx, w, acc_out, up_bias, second, first_low, first_turned, vt, rows_of, sems = rest
    else:
        q, k, v, ctx, w, acc_out, up_bias, vt, rows_of, sems = rest
    rows = x.shape[0]
    pair = q.shape[1]
    copies = [
        pltpu.make_async_copy(message.at[pl.ds(pair, SMALL)], rows_of.at[i], sems.at[8 + i])
        for i, message in enumerate((w0a, w1a))
    ]
    for copy in copies:
        copy.start()
    copies += gather_weights(index, (w0a, w0b, w1a, w1b), w, sems)
    for copy in copies:
        copy.wait()
    biases = []
    for i in range(2):
        parts = rows_of[i].astype(F32)
        biases.append(parts[0:2] + parts[2:4] + parts[4:6])
        up_bias[i : i + 1, :] = biases[i][1:2]
    low = lax.broadcasted_iota(jnp.int32, (1, pair), 1) < pair // 2
    query_bias, value_bias = (
        jnp.where(low, biases[0][0:1, cut], biases[1][0:1, cut])
        for cut in (slice(0, pair), slice(pair, 2 * pair))
    )
    query = (nt(x[...], w[:pair, :]) + query_bias).astype(BF)
    q[...] = (query.astype(F32) * SCALE).astype(BF)
    k[...] = nt(x[...], w[pair : 2 * pair, :]).astype(BF)
    value = (nt(x[...], w[2 * pair : 3 * pair, :]) + value_bias).astype(BF)
    v[...] = value
    vt[...] = value.T

    def span(i, _):
        here = rows_at(i * SPAN, SPAN, SPAN)
        for tile in range(pair // LANES):
            cut = slice(tile * LANES, (tile + 1) * LANES)
            scores = nt(two_heads(k[here, cut]), q[here, cut])
            for h in range(2):
                probs = probs_of(scores[h * SPAN : (h + 1) * SPAN])
                own = slice(tile * LANES + h * HEAD_DIM, tile * LANES + (h + 1) * HEAD_DIM)
                ctx[own, here] = nn(vt[own, here], probs.astype(BF)).astype(BF)
        return 0

    io.push(q, k, v, w)
    lax.fori_loop(0, rows // SPAN, span, 0, unroll=2)
    io.push(ctx)
    total = acc[...] + tn(ctx[...], w[3 * pair :, :])
    acc_out[...] = total
    if last:
        normed, _ = norm_rows(total)
        first = normed * norms[0:1, :] + norms[1:2, :]
        low = first.astype(BF)
        first_low[...] = low
        first_turned[...] = low.T
        second[...] = first + norms[2:3, :]


def attend(index, x, halves, acc, norms=None):
    rows, dim = x.shape
    pair = halves[0].shape[0] - SMALL
    last = norms is not None
    args = [x, *halves, acc] + ([norms] if last else [])
    out = [((rows, pair), BF)] * 3 + [((pair, rows), BF), ((4 * pair, dim), BF), ((rows, dim), F32)]
    out += [((2, dim), F32)]
    if last:
        out += [((rows, dim), F32), ((rows, dim), BF), ((dim, rows), BF)]
    return call(
        functools.partial(attend_body, last),
        index,
        args,
        out,
        [
            pltpu.VMEM((pair, rows), BF),
            pltpu.VMEM((2, SMALL, dim), BF),
            pltpu.SemaphoreType.DMA((10,)),
        ],
        left=(1, 2, 3, 4),
        cold=range(5),
        name="attend",
    )


SMALL = 16


def put_small(message, at, value):
    high = value.astype(BF)
    message[at : at + SMALL, :] = high
    message[at + SMALL : at + 2 * SMALL, :] = (value - high.astype(F32)).astype(BF)


def get_small(message, at):
    return message[at : at + SMALL, :].astype(F32) + message[at + SMALL : at + 2 * SMALL, :].astype(F32)


def attend_scores_body(io, index, grad, w_out, k, q, v, dqt, dk, dv, kt, dc):
    rows, pair = k.shape
    io.need(w_out)
    dc[...] = nt(grad[...], w_out[...]).astype(BF)
    io.need(k, q, v)
    kt[...] = k[...].T

    def span(i, _):
        here = rows_at(i * SPAN, SPAN, SPAN)
        for tile in range(pair // LANES):
            cut = slice(tile * LANES, (tile + 1) * LANES)
            query, grads = q[here, cut], dc[here, cut]
            scores = nt(two_heads(k[here, cut]), query)
            d_probs = nt(two_heads(v[here, cut]), grads)
            low_probs, low_scores = [], []
            for h in range(2):
                own_rows = slice(h * SPAN, (h + 1) * SPAN)
                probs = probs_of(scores[own_rows])
                inner = jnp.sum(d_probs[own_rows] * probs, axis=0, keepdims=True)
                d_scores = (probs * (d_probs[own_rows] - inner)).astype(BF)
                low_probs.append(probs.astype(BF))
                low_scores.append(d_scores)
                mine = slice(tile * LANES + h * HEAD_DIM, tile * LANES + (h + 1) * HEAD_DIM)
                dqt[mine, here] = (nn(kt[mine, here], d_scores) * SCALE).astype(BF)
            dk[here, cut] = of_two_heads(nn(jnp.concatenate(low_scores, axis=0), query)).astype(BF)
            dv[here, cut] = of_two_heads(nn(jnp.concatenate(low_probs, axis=0), grads)).astype(BF)
        return 0

    lax.fori_loop(0, rows // SPAN, span, 0, unroll=2)


def attend_scores(index, kept, grad):
    q, k, v, ctx, w = kept
    rows, pair = q.shape
    return call(
        attend_scores_body,
        index,
        [grad, w, k, q, v],
        [((pair, rows), BF), ((rows, pair), BF), ((rows, pair), BF)],
        [pltpu.VMEM((pair, rows), BF), pltpu.VMEM((rows, pair), BF)],
        far={1: (3 * pair, pair), 2: None, 3: None, 4: None},
        name="attend_scores",
    )


def attend_weights_body(last, io, index, ctx, grad, dqt, dk, dv, x, w, acc, *rest):
    if last:
        small0, small1, *rest = rest
    own, *messages, sums, acc_out = rest
    rows = x.shape[0]
    pair = ctx.shape[0]
    width = pair // 2

    def put(part, value):
        value = value.astype(BF)
        own[part] = value[:width]
        per = 4 // len(messages)
        start = part % per * width
        messages[part // per][start : start + width, :] = value[width:]

    put(0, nn(dqt[...], x[...]))
    put(1, tn(dk[...], x[...]))
    put(2, tn(dv[...], x[...]))
    io.need(ctx)
    put(3, nn(ctx[...], grad[...]))
    ones = jnp.ones((8, rows), BF)
    sum_q, sum_v = nt(ones, dqt[...])[0:1], nn(ones, dv[...])[0:1]
    for block in range(2):
        cut = slice(block * width, (block + 1) * width)
        sums[block : block + 1, 0:width] = sum_q[:, cut]
        sums[block : block + 1, width : 2 * width] = sum_v[:, cut]
    if last:
        for block, small in enumerate((small0, small1)):
            small[6:7, 0:pair] = sums[block : block + 1, :]
        put_small(messages[0], 2 * width, small1[...])
    io.need(w)
    acc_out[...] = (
        acc[...]
        + tn(dqt[...], w[:pair, :])
        + nn(dk[...], w[pair : 2 * pair, :])
        + nn(dv[...], w[2 * pair : 3 * pair, :])
    )


def attend_weights(index, kept, grad, parts, x, acc, small=()):
    rows, dim = x.shape
    pair = kept[3].shape[0]
    width = pair // 2
    last = bool(small)

    def body(io, index, *refs):
        if not last:
            return attend_weights_body(False, io, index, *refs)
        ins, (sums_attn, sums_ffn, sums_far), ups, rest = refs[:8], refs[8:11], refs[11:15], refs[15:]
        outs, out0, spare = rest[:5], rest[5], rest[6]
        for block, out in enumerate((out0, spare)):
            out[...] = jnp.zeros_like(out)
            out[0:3, :] = sums_attn[...]
            out[3:6, :] = sums_ffn[...]
            out[7:8, :] = ups[block][0:1, :]
            out[8:9, 0:pair] = sums_far[block : block + 1, :]
            out[9:10, :] = ups[2 + block][0:1, :]
        return attend_weights_body(True, io, index, *ins, out0, spare, *outs)

    out = [((4, width, dim), BF)]
    out += [((pair + 2 * SMALL, dim), BF), ((pair, dim), BF)] if last else [((2 * pair, dim), BF)]
    out += [((2, pair), F32), ((rows, dim), F32)]
    out += [((SMALL, dim), F32)] if last else []
    return call(
        body,
        index,
        [kept[3], grad, *parts, x, kept[4], acc, *small],
        out,
        [pltpu.VMEM((SMALL, dim), F32)] if last else [],
        far={0: None, 6: (0, 3 * pair)},
        name="attend_weights",
    )


def attend_back_body(last, io, index, ctx, grad, w, x, q, k, v, acc, *rest):
    if last:
        small0, small1, *rest = rest
    own, *messages, sums, acc_out, kt, dc, dqt, dk, dv = rest
    rows = x.shape[0]
    pair = ctx.shape[0]
    width = pair // 2

    def put(part, value):
        value = value.astype(BF)
        own[part] = value[:width]
        per = 4 // len(messages)
        start = part % per * width
        messages[part // per][start : start + width, :] = value[width:]

    io.need(ctx, grad)
    put(3, nn(ctx[...], grad[...]))
    io.need(w, x)
    dc[...] = nt(grad[...], w[3 * pair :, :]).astype(BF)
    io.need(q, k, v)
    kt[...] = k[...].T

    def span(i, _):
        here = rows_at(i * SPAN, SPAN, SPAN)
        for tile in range(pair // LANES):
            cut = slice(tile * LANES, (tile + 1) * LANES)
            query, grads = q[here, cut], dc[here, cut]
            scores = nt(two_heads(k[here, cut]), query)
            d_probs = nt(two_heads(v[here, cut]), grads)
            low_probs, low_scores = [], []
            for h in range(2):
                own_rows = slice(h * SPAN, (h + 1) * SPAN)
                probs = probs_of(scores[own_rows])
                inner = jnp.sum(d_probs[own_rows] * probs, axis=0, keepdims=True)
                d_scores = (probs * (d_probs[own_rows] - inner)).astype(BF)
                low_probs.append(probs.astype(BF))
                low_scores.append(d_scores)
                mine = slice(tile * LANES + h * HEAD_DIM, tile * LANES + (h + 1) * HEAD_DIM)
                dqt[mine, here] = (nn(kt[mine, here], d_scores) * SCALE).astype(BF)
            dk[here, cut] = of_two_heads(nn(jnp.concatenate(low_scores, axis=0), query)).astype(BF)
            dv[here, cut] = of_two_heads(nn(jnp.concatenate(low_probs, axis=0), grads)).astype(BF)
        return 0

    lax.fori_loop(0, rows // SPAN, span, 0, unroll=2)
    put(0, nn(dqt[...], x[...]))
    put(1, tn(dk[...], x[...]))
    put(2, tn(dv[...], x[...]))
    ones = jnp.ones((8, rows), BF)
    sum_q, sum_v = nt(ones, dqt[...])[0:1], nn(ones, dv[...])[0:1]
    for block in range(2):
        cut = slice(block * width, (block + 1) * width)
        sums[block : block + 1, 0:width] = sum_q[:, cut]
        sums[block : block + 1, width : 2 * width] = sum_v[:, cut]
    if last:
        for block, small in enumerate((small0, small1)):
            small[6:7, 0:pair] = sums[block : block + 1, :]
        put_small(messages[0], 2 * width, small1[...])
    acc_out[...] = (
        acc[...]
        + tn(dqt[...], w[:pair, :])
        + nn(dk[...], w[pair : 2 * pair, :])
        + nn(dv[...], w[2 * pair : 3 * pair, :])
    )


def attend_back(index, kept, grad, x, acc, small=()):
    rows, dim = x.shape
    pair = kept[3].shape[0]
    width = pair // 2
    last = bool(small)

    def body(io, index, *refs):
        if not last:
            return attend_back_body(False, io, index, *refs)
        ins, (sums_attn, sums_ffn, sums_far), ups, rest = refs[:8], refs[8:11], refs[11:15], refs[15:]
        outs, out0, spare, scratch = rest[:5], rest[5], rest[6], rest[7:]
        for block, out in enumerate((out0, spare)):
            out[...] = jnp.zeros_like(out)
            out[0:3, :] = sums_attn[...]
            out[3:6, :] = sums_ffn[...]
            out[7:8, :] = ups[block][0:1, :]
            out[8:9, 0:pair] = sums_far[block : block + 1, :]
            out[9:10, :] = ups[2 + block][0:1, :]
        return attend_back_body(True, io, index, *ins, out0, spare, *outs, *scratch)

    out = [((4, width, dim), BF)]
    out += [((pair + 2 * SMALL, dim), BF), ((pair, dim), BF)] if last else [((2 * pair, dim), BF)]
    out += [((2, pair), F32), ((rows, dim), F32)]
    out += [((SMALL, dim), F32)] if last else []
    return call(
        body,
        index,
        [kept[3], grad, kept[4], x, *kept[:3], acc, *small],
        out,
        ([pltpu.VMEM((SMALL, dim), F32)] if last else [])
        + [pltpu.VMEM((pair, rows), BF), pltpu.VMEM((rows, pair), BF)]
        + [pltpu.VMEM((pair, rows), BF)]
        + [pltpu.VMEM((rows, pair), BF), pltpu.VMEM((rows, pair), BF)],
        far=(0, 2, 4, 5, 6),
        name="attend_back",
    )


def gelu_parts(upper):
    phi = 0.5 * (1.0 + lax.erf(upper * SQRT_HALF))
    slope = phi + upper * jnp.exp(-0.5 * upper * upper) * INV_ROOT_TWO_PI
    return (upper * phi).astype(BF), slope.astype(BF)


def feed_body(count, io, index, first, *refs):
    weights, acc, bias, refs = refs[: 2 * count], refs[2 * count], refs[2 * count + 1], refs[2 * count + 2 :]
    active, slope, acc_out = refs[:count], refs[count : 2 * count], refs[2 * count]
    total = None
    for i in range(count):
        up, down = weights[2 * i : 2 * i + 2]
        size = up.shape[1]
        step = min(size, 384)
        for at in range(0, size, step):
            cut = slice(at, at + step)
            act, slp = gelu_parts(nn(first[...], up[:, cut]) + bias[i : i + 1, cut])
            active[i][cut, :] = act.T
            slope[i][:, cut] = slp
            more = nn(act, down[cut, :])
            total = more if total is None else total + more
        io.push(active[i], slope[i])
    acc_out[...] = total + acc[...]


def feed(index, first, acc, bias, up, down):
    rows, dim = first.shape
    count, size = len(up), up[0].shape[1]
    out = call(
        functools.partial(feed_body, count),
        index,
        [first, *(t for both in zip(up, down) for t in both), acc, bias],
        [((size, rows), BF)] * count + [((rows, size), BF)] * count + [((rows, dim), F32)],
        name="feed",
    )
    return out[:count], out[count : 2 * count], out[2 * count]


def x_half(index, h, size):
    return rows_at((index[0] if h == 0 else 1 - index[0]) * size, size, LANES)


def feed_up_body(block, io, index, first, *refs):
    up, bias, plain, active, slope = refs[:2], refs[2], refs[3:5], refs[5:7], refs[7:9]
    for h in range(2):
        there = x_half(index, h, up[h].shape[1])
        act, slp = gelu_parts(nn(first[...], up[h][: first.shape[1], :]) + bias[block : block + 1, there])
        plain[h][...] = act
        active[h][...] = act.T
        slope[h][...] = slp


def feed_up(index, first, bias, block, up):
    rows, dim = first.shape
    size = up[0].shape[1]
    out = call(
        functools.partial(feed_up_body, block),
        index,
        [first, *up, bias],
        [((rows, size), BF)] * 2 + [((size, rows), BF)] * 2 + [((rows, size), BF)] * 2,
        name="feed_up",
    )
    return out[:2], out[2:4], out[4:]


def down_dot(index, active, down):
    size = active[0].shape[1]
    first, second = (nn(active[h][...], down[x_half(index, h, size), :]) for h in range(2))
    return first + second


def feed_down(index, acc, active, down):
    def body(io, index, acc, first, second, down, out):
        out[...] = acc[...] + down_dot(index, (first, second), down)

    return call(body, index, [acc, *active, down], [(acc.shape, F32)], name="feed_down")[0]


def down_back_body(near, more, last, io, index, grad, *refs):
    count = 1 if near else 2
    active, refs = refs[:count], refs[count:]
    other, refs = (refs[0], refs[1:]) if more else (None, refs)
    far, refs = (refs[0], refs[1:]) if last else (None, refs)
    out, refs = refs[0], refs[1:]
    half = (out if last else out.at[0]).shape[0]
    if last:
        send, sems = refs
        copy = pltpu.make_async_copy(far.at[1], send.at[0], sems.at[0])
        copy.start()
    for h in range(2):
        if near:
            start = (index[0] if h == 0 else 1 - index[0]) * half
            value = nn(active[0][rows_at(start, half, LANES), :], grad[...])
        else:
            value = nn(active[h][...], grad[...])
        if more:
            value = value + other[h].astype(F32)
        if last and h == 0:
            out[...] = value.astype(BF)
        elif last:
            send[1] = value.astype(BF)
        else:
            out[h] = value.astype(BF)
    if last:
        copy.wait()


def down_back(index, grad, active, other=None, far=None):
    rows, dim = grad.shape
    near = len(active) == 1
    units = sum(t.shape[0] for t in active)
    more, last = other is not None, far is not None
    parts = (2, units // 2, dim)
    args = [grad, *active] + ([other] if more else []) + ([far] if last else [])
    return call(
        functools.partial(down_back_body, near, more, last),
        index,
        args,
        [((units // 2, dim), BF), (parts, BF)] if last else [(parts, BF)],
        [pltpu.SemaphoreType.DMA((1,))] if last else [],
        left=[len(args) - 1] if last else [],
        name="down_back",
    )


def up_back_body(near, more, apart, io, index, grad, *refs):
    count = 1 if near else 2
    down, slope, refs = refs[0], refs[1 : 1 + count], refs[1 + count :]
    first_turned, up, refs = refs[0], refs[1 : 1 + count], refs[1 + count :]
    other, refs = (refs[:2], refs[2:]) if more else ((), refs)
    acc, refs = refs[0], refs[1:]
    g_up, refs = (refs[:2], refs[2:]) if apart else ((refs[0].at[0], refs[0].at[1]), refs[1:])
    sums, acc_out = refs
    half = sums.shape[1] // 2
    size = first_turned.shape[0] // 2
    ones = jnp.ones((8, grad.shape[0]), BF)
    total = acc[...]
    if near:
        d_upper = (nt(grad[...], down[...]) * wide(slope[0][...])).astype(BF)
        sums[...] = nn(ones, d_upper)
        for z in range(2):
            rows = rows_at((index[1] if z == 0 else 1 - index[1]) * size, size, LANES)
            value = nn(first_turned[rows, :], d_upper)
            for h in range(2):
                cut = slice(h * half, (h + 1) * half)

                @pl.when(index[0] == 0)
                def _():
                    own = value[:, cut]
                    if more:
                        own = own + other[z][:, cut].astype(F32)
                    g_up[z][:, cut] = own.astype(BF)

                @pl.when(index[0] == 1)
                def _():
                    own = value[:, (1 - h) * half : (2 - h) * half]
                    if more:
                        own = own + other[z][:, cut].astype(F32)
                    g_up[z][:, cut] = own.astype(BF)

        acc_out[...] = total + nt(d_upper, up[0][...])
        return
    for h in range(2):
        there = x_half(index, h, half)
        cut = slice(h * half, (h + 1) * half)
        slp = wide(slope[h][...])
        d_upper = (nt(grad[...], down[there, :]) * slp).astype(BF)
        sums[:, there] = nn(ones, d_upper)
        for z in range(2):
            rows = rows_at((index[1] if z == 0 else 1 - index[1]) * size, size, LANES)
            value = nn(first_turned[rows, :], d_upper)
            if more:
                value = value + other[z][:, cut].astype(F32)
            g_up[z][:, cut] = value.astype(BF)
        total = total + nt(d_upper, up[h][: acc.shape[1], :])
    acc_out[...] = total


def up_back(index, first_turned, grad, acc, slope, up, down, other=(), apart=False):
    rows, dim = grad.shape
    near = len(up) == 1
    units = down.shape[0]
    half = (dim // 2, units)
    *got, sums, total = call(
        functools.partial(up_back_body, near, bool(other), apart),
        index,
        [grad, down, *slope, first_turned, *up, *other, acc],
        ([(half, BF)] * 2 if apart else [((2, *half), BF)])
        + [((8, units), F32), ((rows, dim), F32)],
        name="up_back",
    )
    return got, sums, total


def pack_body(io, index, qkv, output, w_up, biases, first, second, up_half, sems):
    width = output.shape[0]
    there = rows_at(index[0] * up_half.shape[1], up_half.shape[1], LANES)
    up_copy = pltpu.make_async_copy(
        w_up.at[:, there], up_half.at[pl.ds(0, w_up.shape[0])], sems.at[4]
    )

    def copies(x):
        for part in range(4):
            source = output if part == 3 else qkv.at[pl.ds(part * width, width)]
            place = first if part // 2 == x else second
            place = place.at[pl.ds(part % 2 * width, width)]
            yield pltpu.make_async_copy(source, place, sems.at[part])

    for x in range(2):

        @pl.when(index[0] == x)
        def _():
            for copy in copies(x):
                copy.start()
            up_copy.start()
            rest = biases[...]
            parts = []
            for _ in range(3):
                parts.append(rest.astype(BF).astype(F32))
                rest = rest - parts[-1]
            parts.append(jnp.zeros((SMALL - 6, rest.shape[1]), F32))
            first[2 * width :, :] = jnp.concatenate(parts, axis=0).astype(BF)
            for copy in copies(x):
                copy.wait()
            up_copy.wait()


def pack(index, qkv, output, w_up, biases):
    width, dim = output.shape
    out = [((2 * width + SMALL, dim), BF), ((2 * width, dim), BF), ((dim + 32, w_up.shape[1] // 2), BF)]
    return call(
        pack_body,
        index,
        [qkv, output, w_up, biases],
        out,
        [pltpu.SemaphoreType.DMA((5,))],
        left=(0, 1, 2),
        still=True,
        name="pack",
    )


def turn_body(io, index, first, second, down, acc, out_grad, cls_rows, norms, *refs):
    mixed, d_second, low, sums = refs
    second = acc[...] + down_dot(index, (first, second), down)
    normed, factor = norm_rows(second)
    mixed[...] = (normed * norms[0:1, :] + norms[1:2, :]).astype(BF)
    spans = cls_rows.shape[0]
    shape = (spans, SPAN, out_grad.shape[1])
    first_row = lax.broadcasted_iota(jnp.int32, shape, 1) == 0
    incoming = wide(out_grad[...]).reshape(shape)
    incoming = incoming + jnp.where(first_row, cls_rows[...][:, None, :], 0.0)
    incoming = incoming.reshape(out_grad.shape)
    grad = norm_back(incoming, normed, factor, norms[0:1, :])
    d_second[...] = grad
    low[...] = grad.astype(BF)
    sums[0:1, :] = jnp.sum(incoming * normed, axis=0, keepdims=True)
    sums[1:2, :] = jnp.sum(incoming, axis=0, keepdims=True)
    sums[2:3, :] = jnp.sum(grad.astype(BF).astype(F32), axis=0, keepdims=True)


def turn(index, acc, cotangent, norms, active, down):
    size = acc.shape
    return call(
        turn_body,
        index,
        [*active, down, acc, *cotangent, norms],
        [(size, BF), (size, F32), (size, BF), ((3, size[1]), F32)],
        name="turn",
    )


def first_back_body(io, index, attended, incoming, norms, d_attn, low, sums):
    normed, factor = norm_rows(attended[...])
    grad = norm_back(incoming[...], normed, factor, norms[0:1, :])
    d_attn[...] = grad
    low[...] = grad.astype(BF)
    sums[0:1, :] = jnp.sum(incoming[...] * normed, axis=0, keepdims=True)
    sums[1:2, :] = jnp.sum(incoming[...], axis=0, keepdims=True)
    sums[2:3, :] = jnp.sum(grad.astype(BF).astype(F32), axis=0, keepdims=True)


def first_back(index, attended, incoming, norms):
    size = attended.shape
    return call(
        first_back_body,
        index,
        [attended, incoming, norms],
        [(size, F32), (size, BF), ((3, size[1]), F32)],
        name="first_back",
    )


def wide(value):
    return value.astype(F32)


def blocks(index, args, out, body, name="blocks", cold=()):
    def run(io, index, *refs):
        body(index, refs[: len(args)], refs[len(args) :])

    return call(run, index, args, out, cold=cold, name=name)


def sums(index, *groups):
    def body(_, ins, outs):
        at = 0
        for group, out in zip(groups, outs):
            total = wide(ins[at][...])
            for i in range(1, len(group)):
                total = total + wide(ins[at + i][...])
            out[...] = total.astype(BF)
            at += len(group)

    return blocks(
        index,
        [a for group in groups for a in group],
        [(group[0].shape, BF) for group in groups],
        body,
        name="sums",
    )


def split_sum(index, which, a, b):
    half = a.shape[0] // 2

    def body(index, ins, outs):
        for out, bit in zip(outs, (index[which], 1 - index[which])):
            there = rows_at(bit * half, half)
            out[...] = (wide(ins[0][there, :]) + wide(ins[1][there, :])).astype(BF)

    return blocks(index, [a, b], [((half, a.shape[1]), BF)] * 2, body, name="split_sum")


def join(index, which, own, other):
    half = own.shape[0]

    def body(index, ins, outs):
        for value, bit in zip(ins, (index[which], 1 - index[which])):
            outs[0][rows_at(bit * half, half), :] = value[...]

    return blocks(index, [own, other], [((2 * half, own.shape[1]), BF)], body, name="join")[0]


def swap(value, axis, bit):
    size = lax.axis_size(axis)
    return lax.ppermute(value, axis, [(i, i ^ bit) for i in range(size)])


class Order:
    def __init__(self, token):
        self.token = token

    def __call__(self, *values):
        self.token, *values = lax.optimization_barrier((self.token, *values))
        return values[0] if len(values) == 1 else values


STEPS = (None, "D", None, "UDQVDVUQDVUVQDQUVQQUDVVUQ")
PATHS = {"D": "xz", "U": "yz", "Q": "xz", "V": "Z"}


def pick_half(value, index, axis=0):
    half = value.shape[axis] // 2
    return lax.dynamic_slice_in_dim(value, index * half, half, axis)


def local(
    inputs,
    w_qkv,
    bias_query,
    bias_value,
    w_output,
    bias_output,
    gain_attn,
    shift_attn,
    w_up,
    bias_up,
    w_down,
    bias_down,
    gain_ffn,
    shift_ffn,
    out_grad,
    mlm_mask,
    span_doc,
    cls_grad,
):
    rows, dim = inputs.shape
    width = w_qkv.shape[2]
    units = w_up.shape[1]
    half = units // 2
    dp = lax.axis_index("dp")
    bits = [1 << i for i in range(lax.axis_size("dp").bit_length() - 1)]
    ix = dp % 2
    scalars = jnp.stack([ix, (dp // bits[1]) % 2, (dp // bits[2]) % 2]).astype(jnp.int32)
    index = Kernels(scalars, jnp.zeros((8, LANES), F32))
    order = Order(bias_output)

    def core(value):
        return swap(value, "tensor", CORE)

    def over_y(value):
        return swap(value, "tensor", Y)

    def over(value, n):
        return swap(value, "dp", bits[n])

    biases = jnp.concatenate([bias_query, bias_query, bias_value, bias_value, bias_up])
    *own, up_send = pack(
        index,
        w_qkv.transpose(1, 2, 0).reshape(3 * width, dim),
        w_output,
        w_up,
        biases.reshape(2, dim),
    )
    attn = {0: tuple(own)}
    attn_a = over_y(own[0])
    attn[1] = tuple(core(t) for t in own)
    up_a = over_y(up_send)

    norms_attn = jnp.stack([gain_attn, shift_attn, bias_down])
    norms_ffn = jnp.stack([gain_ffn, shift_ffn])
    kept = {}
    attended = bias_output + inputs.astype(F32)

    weighting = jnp.where(mlm_mask == 1, 2.0, 0.5).astype(BF)
    docs_here = cls_grad.shape[0]
    local_doc = span_doc - dp * docs_here
    picker = (local_doc[:, None] == jnp.arange(docs_here, dtype=jnp.int32)[None, :]).astype(F32)
    cls_rows = jnp.dot(picker, cls_grad.astype(F32), precision=lax.Precision.HIGHEST)
    cotangent = [out_grad * weighting[:, None], cls_rows]

    up, down = {0: w_up, 1: core(w_up)}, {0: w_down, 1: core(w_down)}
    near = order(*attn[0], *attn[1], attended)
    attn[0], attn[1], attended = tuple(near[:2]), tuple(near[2:4]), near[4]
    *kept[0], attended, up_bias = attend(index, inputs, attn[0] + attn[1], attended)

    attended, attn_a, up[1], down[1], w_down, *cotangent = order(
        attended, attn_a, up[1], down[1], w_down, *cotangent
    )
    attn_b = over(attn_a, 0)
    far_a = core(attn_a)
    down[2] = over_y(w_down)
    up_a = order(up_a)
    up_b = over(up_a, 0)
    up_far_a = core(up_a)
    attn_b, far_a = order(attn_b, far_a)
    far_b, up_far_a = order(core(attn_b), up_far_a)
    attn[2], attn[3] = (attn_a, attn_b), (far_a, far_b)
    *kept[2], attended, up_bias_far, second, first_low, first_turned = attend(
        index, inputs, attn[2] + attn[3], attended, norms_attn
    )

    act_near, slope_near, second = feed(
        index, first_low, second, up_bias, [up[0], up[1]], [down[0], down[1]]
    )
    second, up_b = order(second, up_b)
    up_far_b = core(up_b)
    plain_2, act_2, slope_2 = feed_up(index, first_low, up_bias_far, 0, [up_a, up_b])
    *plain_2, down[2] = order(*plain_2, down[2])
    down[3] = core(down[2])
    second, up_far_b = order(feed_down(index, second, plain_2, down[2]), up_far_b)
    plain_3, act_3, slope_3 = feed_up(index, first_low, up_bias_far, 1, [up_far_a, up_far_b])
    *plain_3, down[3] = order(*plain_3, down[3])
    mixed, d_second, branch_grad, sums_ffn = turn(
        index, second, cotangent, norms_ffn, plain_3, down[3]
    )

    g_bias_up = {}
    act_of = [[act_near[0]], [act_near[1]], act_2, act_3]
    slope_of = [[slope_near[0]], [slope_near[1]], slope_2, slope_3]
    up_of = [[up[0]], [up[1]], [up_a, up_b], [up_far_a, up_far_b]]

    def back_up(r, total, other=(), apart=False):
        got, g_bias_up[r], total = up_back(
            index, first_turned, branch_grad, total, slope_of[r], up_of[r], down[r], other, apart
        )
        return order(*got, total)

    def add(*values):
        total = wide(values[0])
        for value in values[1:]:
            total = total + wide(value)
        return total.astype(BF)

    def more(value):
        for n in range(3, len(bits)):
            value = sums(index, [value, over(value, n)])[0]
        return value

    def run(name, args, out, body):
        dtypes = [(t[:-1], F32) if t[-1] == F32 else (t, BF) for t in out]
        cold = range(len(out)) if name.endswith("_out") else ()
        return order(*blocks(index, args, dtypes, body, name=name, cold=cold))

    def both(index, n):
        return index[n], 1 - index[n]

    part = width // 2
    extra = 2 * SMALL
    rows_small = (SMALL, dim, F32)
    result = {}

    def down_sum():
        size = half // 2
        quarter = (size, dim)

        def down_1(index, ins, outs):
            far, near, came = ins
            for i, bit in enumerate(both(index, 1)):
                there = rows_at(bit * size, size)
                for j, mine in enumerate((far.at[0], near)):
                    place = outs[j] if i == 0 else outs[2].at[j]
                    place[...] = add(mine[there, :], came[j, there, :])

        def down_2(_, ins, outs):
            for i in range(2):
                outs[i][...] = add(ins[i][...], ins[2][i])

        def down_out(index, ins, outs):
            for ref, x in zip(ins, both(index, 0)):
                outs[0][rows_at(x * half, half), :] = wide(ref[...])

        def down_1y(_, ins, outs):
            far, near, came = ins
            outs[0][...] = add(far[0], came[0])
            outs[1][...] = add(near[...], came[1])

        came = yield over(down_send, 0)
        if PATHS["D"] == "xz":
            f, n, s = run(
                "down_1", [far_down, near_down, came], [quarter, quarter, (2, *quarter)], down_1
            )
            came = yield over(s, 1)
            f, n = run("down_2", [f, n, came], [quarter] * 2, down_2)
            came = yield over_y(f)
            t = order(*sums(index, [n, came]))
        else:
            f, n = run("down_1", [far_down, near_down, came], [(half, dim)] * 2, down_1y)
            came = yield over_y(f)
            k, s = order(*split_sum(index, 1, n, came))
            came = yield over(s, 1)
            t = order(*sums(index, [k, came]))
        came = yield over(t, 2)
        t = order(more(*sums(index, [t, came])))
        came = yield over(t, 1)
        t = order(join(index, 1, t, came))
        came = yield over(t, 0)
        result["down"] = run("down_out", [t, came], [(units, dim, F32)], down_out)

    def up_sum():
        def up_1(_, ins, outs):
            for i in range(2):
                outs[i][...] = add(ins[0][i], ins[1][i])

        def up_2(_, ins, outs):
            for out, cut in zip(outs, (slice(0, half), slice(half, None))):
                out[...] = add(ins[0][:, cut], ins[1][:, cut])

        def up_5(_, ins, outs):
            for i in range(2):
                outs[0][:, i * half : (i + 1) * half] = ins[i][...]

        def up_out(index, ins, outs):
            for ref, z in zip(ins, both(index, 1)):
                rows_here = rows_at(z * (dim // 2), dim // 2)
                for h, x in enumerate(both(index, 0)):
                    outs[0][rows_here, rows_at(x * half, half, LANES)] = wide(
                        ref[:, h * half : (h + 1) * half]
                    )

        def up_1x(_, ins, outs):
            for i in range(2):
                for out, cut in zip(outs, (slice(0, half), slice(half, None))):
                    out[i] = add(ins[0][i, :, cut], ins[1][i, :, cut])

        def up_5x(_, ins, outs):
            for i in range(2):
                outs[0][i] = ins[i][...]

        def up_out_x(index, ins, outs):
            for ref, x in zip(ins, both(index, 0)):
                for i, z in enumerate(both(index, 1)):
                    outs[0][rows_at(z * (dim // 2), dim // 2), rows_at(x * half, half, LANES)] = wide(
                        ref[i]
                    )

        came = yield over_y(far_up)
        if PATHS["U"] == "yx":
            pair_of = (2, dim // 2, half)
            k, s = run("up_1", [near_up, came], [pair_of] * 2, up_1x)
            came = yield over(s, 0)
            k, s = run("up_2", [k, came], [pair_of[1:]] * 2, up_1)
            came = yield over(s, 1)
            t = order(*sums(index, [k, came]))
            came = yield over(t, 2)
            t = order(more(*sums(index, [t, came])))
            came = yield over(t, 1)
            t = run("up_5", [t, came], [pair_of], up_5x)
            came = yield over(t, 0)
            result["up"] = run("up_out", [t, came], [(dim, units, F32)], up_out_x)
            return
        k, s = run("up_1", [near_up, came], [(dim // 2, units)] * 2, up_1)
        came = yield over(s, 1)
        k, s = run("up_2", [k, came], [(dim // 2, half)] * 2, up_2)
        came = yield over(s, 0)
        t = order(*sums(index, [k, came]))
        came = yield over(t, 2)
        t = order(more(*sums(index, [t, came])))
        came = yield over(t, 0)
        t = run("up_5", [t, came], [(dim // 2, units)], up_5)
        came = yield over(t, 1)
        result["up"] = run("up_out", [t, came], [(dim, units, F32)], up_out)

    def rows_of(part):
        return slice(part * width, (part + 1) * width)

    def qk_sum(far, near, far_came, near_came, little):
        def qk_1(index, ins, outs):
            far, near, far_came, near_came, little = ins
            for i, bit in enumerate(both(index, 0)):
                for j, (mine, came) in enumerate(((far, far_came), (near, near_came))):
                    for k in range(2):

                        @pl.when(bit == k)
                        def _():
                            value = add(mine[k], came[rows_of(k), :])
                            if i == 0:
                                outs[j][...] = value
                            else:
                                outs[2][rows_of(j), :] = value

            total = little[...] + get_small(near_came, 2 * width)
            outs[3][...] = total
            put_small(outs[2], 2 * width, total)

        def qk_2(index, ins, outs):
            far, near, came, little = ins
            for i, bit in enumerate(both(index, 1)):
                there = rows_at(bit * part, part)
                for j, mine in enumerate((far, near)):
                    value = add(mine[there, :], came[rows_at(j * width + bit * part, part), :])
                    if i == 0:
                        outs[j][...] = value
                    else:
                        outs[2][j * part : (j + 1) * part, :] = value
            total = little[...] + get_small(came, 2 * width)
            outs[3][...] = total
            put_small(outs[2], 2 * part, total)

        def qk_3(_, ins, outs):
            far, near, came, little = ins
            outs[0][:part, :] = add(far[...], came[:part, :])
            outs[1][...] = add(near[...], came[part : 2 * part, :])
            total = little[...] + get_small(came, 2 * part)
            outs[2][...] = total
            outs[3][...] = jnp.zeros_like(total)
            outs[3][0:6, :] = total[0:6]
            outs[3][6:8, :] = total[8:10]
            put_small(outs[0], part, outs[3][...])

        def qk_4(_, ins, outs):
            mine, came, little = ins
            outs[0][:part, :] = add(mine[...], came[:part, :])
            total = little[...] + get_small(came, part)
            outs[1][...] = total
            put_small(outs[0], part, total)

        def qk_5(_, ins, outs):
            mine, came, little = ins
            outs[0][...] = add(mine[:part, :], came[:part, :])
            outs[1][...] = little[...] + get_small(came, part)

        near_came = yield near_came
        f, n, s, little = run(
            "qk_1",
            [far, near, far_came, near_came, little],
            [(width, dim), (width, dim), (2 * width + extra, dim), rows_small],
            qk_1,
        )
        def qk_2y(_, ins, outs):
            far, near, came, little = ins
            outs[0][:width, :] = add(far[...], came[rows_of(0), :])
            outs[1][...] = add(near[...], came[rows_of(1), :])
            total = little[...] + get_small(came, 2 * width)
            outs[2][...] = total
            outs[3][...] = jnp.zeros_like(total)
            outs[3][0:6, :] = total[0:6]
            outs[3][6:8, :] = total[8:10]
            put_small(outs[0], width, outs[3][...])

        def qk_3y(index, ins, outs):
            mine, came, little = ins
            for bit, out in zip(both(index, 1), outs):
                there = rows_at(bit * part, part)
                out[:part, :] = add(mine[there, :], came[there, :])
            total = little[...] + get_small(came, width)
            outs[2][...] = total
            put_small(outs[1], part, total)

        came = yield over(s, 0)
        if PATHS["Q"] == "xy":
            f, n, little, _ = run(
                "qk_2",
                [f, n, came, little],
                [(width + extra, dim), (width, dim), rows_small, rows_small],
                qk_2y,
            )
            came = yield over_y(f)
            k, s, little = run(
                "qk_3", [n, came, little], [(part, dim), (part + extra, dim), rows_small], qk_3y
            )
            came = yield over(s, 1)
            t, little = run("qk_4", [k, came, little], [(part + extra, dim), rows_small], qk_4)
            came = yield over(t, 2)
            t, little = run("qk_5", [t, came, little], [(part, dim), rows_small], qk_5)
            t = more(t)
            for n in range(3, len(bits)):
                little = little + over(little, n)
            result["little"] = little
            came = yield over(t, 1)
            t = order(join(index, 1, t, came))
            came = yield over(t, 0)
            result["qk"] = (t, came)
            return
        f, n, s, little = run(
            "qk_2",
            [f, n, came, little],
            [(part, dim), (part, dim), (2 * part + extra, dim), rows_small],
            qk_2,
        )
        came = yield over(s, 1)
        f, n, little, _ = run(
            "qk_3",
            [f, n, came, little],
            [(part + extra, dim), (part, dim), rows_small, rows_small],
            qk_3,
        )
        came = yield over_y(f)
        t, little = run("qk_4", [n, came, little], [(part + extra, dim), rows_small], qk_4)
        came = yield over(t, 2)
        t, little = run("qk_5", [t, came, little], [(part, dim), rows_small], qk_5)
        t = more(t)
        for n in range(3, len(bits)):
            little = little + over(little, n)
        result["little"] = little
        came = yield over(t, 1)
        t = order(join(index, 1, t, came))
        came = yield over(t, 0)
        result["qk"] = (t, came)

    def vo_sum(far, near, far_came, near_came):
        def vo_1(_, ins, outs):
            far, near, far_came, near_came = ins
            for k in range(2):
                outs[0][rows_of(k), :] = add(far[2 + k], far_came[rows_of(2 + k), :])
                outs[1][rows_of(k), :] = add(near[2 + k], near_came[rows_of(k), :])

        near_came = yield near_came
        f, n = run("vo_1", [far, near, far_came, near_came], [(2 * width, dim)] * 2, vo_1)
        f = yield f
        came = yield over_y(f)
        k, s = order(*split_sum(index, 0, n, came))
        came = yield over(s, 0)
        if PATHS["V"] == "R":
            k, s = order(*split_sum(index, 1, k, came))
            came = yield over(s, 1)
            t = order(*sums(index, [k, came]))
            came = yield over(t, 2)
            t = order(more(*sums(index, [t, came])))
            came = yield over(t, 1)
            t = order(join(index, 1, t, came))
            came = yield over(t, 0)
            result["vo"] = (t, came)
            return
        t = order(*sums(index, [k, came]))
        came = yield over(t, 1)
        t = order(*sums(index, [t, came]))
        came = yield over(t, 2)
        t = order(more(*sums(index, [t, came])))
        came = yield over(t, 0)
        result["vo"] = (t, came)

    chains, waiting = {}, {}

    def start(name, chain):
        chains[name] = chain
        waiting[name] = next(chain)

    def go(names, arrived=None):
        for name in names:
            if name not in waiting:
                continue
            value = waiting.pop(name) if arrived else order(waiting.pop(name))
            try:
                waiting[name] = chains[name].send(value)
            except StopIteration:
                pass

    down_3 = core(order(*down_back(index, branch_grad, act_of[3])))
    down_1 = core(order(*down_back(index, branch_grad, act_of[1])))
    *up_3, d_first = back_up(3, d_second, apart=True)
    up_3 = [core(t) for t in up_3]
    down_3 = order(down_3)
    far_down = order(*down_back(index, branch_grad, act_of[2], down_3))
    down_1 = order(down_1)
    near_down, down_send = order(*down_back(index, branch_grad, act_of[0], down_1, far_down))
    start("D", down_sum())
    *up_1, d_first = back_up(1, order(d_first), apart=True)
    up_3 = order(*up_3)
    up_1 = [core(t) for t in up_1]
    far_up, d_first = back_up(2, d_first, up_3)
    start("U", up_sum())
    up_1 = order(*up_1)
    near_up, d_first = back_up(0, d_first, up_1)

    d_attn, attended_grad, sums_attn = first_back(index, attended, d_first, norms_attn)

    def attention_back(r, total, between, small=()):
        if between is None:
            return order(*attend_back(index, kept[r], attended_grad, inputs, total, small))
        parts = order(*attend_scores(index, kept[r], attended_grad))
        go(between)
        *parts, total = order(*parts, total)
        out = order(*attend_weights(index, kept[r], attended_grad, parts, inputs, total, small))
        return out

    far_attn, *messages, sums_far, input_grad = attention_back(2, d_attn, STEPS[0])
    waiting["D"], input_grad, *messages = order(waiting["D"], input_grad, *messages)
    from_core = [core(t) for t in messages]
    go("D", True)
    input_grad = order(input_grad)
    near_attn, *to_core, _, input_grad, little = attention_back(
        0,
        input_grad,
        STEPS[2],
        (sums_attn, sums_ffn, sums_far, *(g_bias_up[r] for r in range(4))),
    )
    to_core = [core(t) for t in to_core]
    if STEPS[3][0] in waiting:
        from_core, waiting[STEPS[3][0]] = order(*from_core, waiting[STEPS[3][0]])
    else:
        from_core = order(*from_core)
    start("Q", qk_sum(far_attn, near_attn, from_core, to_core[0], little))
    start("V", vo_sum(far_attn, near_attn, from_core, to_core[1]))
    go(STEPS[3])
    while waiting:
        go([*waiting])

    def attn_out(index, ins, outs):
        qk, vo = ins[:2], ins[2:]
        for ref, x in zip(qk, both(index, 0)):
            outs[0][rows_at(x * width, width), :] = wide(ref[...])
        for x in range(2):

            @pl.when(index[0] == x)
            def _():
                outs[0][rows_of(2), :] = wide(vo[x][...])
                outs[1][...] = wide(vo[1 - x][...])

    grad_down, grad_up, little = result["down"], result["up"], result["little"]
    grad_qkv, grad_output = run(
        "attn_out",
        [*result["qk"], *result["vo"]],
        [(3 * width, dim, F32), (width, dim, F32)],
        attn_out,
    )
    grad_qkv = grad_qkv.reshape(3, width, dim).transpose(2, 0, 1)
    return (
        mixed,
        input_grad,
        grad_qkv,
        little[6, :width],
        little[6, width : 2 * width],
        grad_output,
        little[2],
        little[0],
        little[1],
        grad_up,
        little[7],
        grad_down,
        little[5],
        little[3],
        little[4],
    )


def solution(mesh):
    return jax.shard_map(
        local,
        mesh=mesh,
        in_specs=(
            P(("dp", "tensor"), None),
            P(None, None, "tensor"),
            P("tensor"),
            P("tensor"),
            P("tensor", None),
            P(),
            P(),
            P(),
            P(None, "tensor"),
            P("tensor"),
            P("tensor", None),
            P(),
            P(),
            P(),
            P(("dp", "tensor"), None),
            P(("dp", "tensor")),
            P(("dp", "tensor")),
            P("dp", None),
        ),
        out_specs=(
            P(("dp", "tensor"), None),
            P(("dp", "tensor"), None),
            P(None, None, "tensor"),
            P("tensor"),
            P("tensor"),
            P("tensor", None),
            P(),
            P(),
            P(),
            P(None, "tensor"),
            P("tensor"),
            P("tensor", None),
            P(),
            P(),
            P(),
        ),
        check_vma=False,
    )
```
